32 devices in a mesh: groups: 2 (over y), row: 4 (over x, core), col: 4 (over z).
Axes of the slice: x: 2, y: 2, z: 4, core: 2. Of those that a mesh axis runs over, the one named last changes fastest.
Arguments:
- corpus: float32 [65536, 256], P(('groups', 'row', 'col')), parts along dimension 0, may hold values from -20 to 20
- sample_rows: int32 [8192], P(('groups', 'row', 'col')), parts along dimension 0, may hold values from 0 to 2047
- initial: float32 [64, 8192], P(None, ('groups', 'row', 'col')), parts along dimension 1, may hold values from -6 to 6
Outputs:
- vectors: float32 [64, 8192], P(None, ('groups', 'row', 'col')), parts along dimension 1
The draws below stay inside these ranges and needn't reach their ends.
There are 2 independent parts, one for each index of `groups`. The reference program is written for one: setup_inputs(seed, part) draws one part's arguments, and reference() takes and returns one part's arrays. A program takes and returns all parts, laid end to end along the dimension named above; each array names one. Nothing has to cross between parts.
Inputs may be any that keep to these rules, and one draw needn't show every extreme that they name: Every device samples its landmarks from its own block of corpus rows: landmark i is corpus row (i // 256) * 2048 + sample_rows[i]; repeats may occur.
All inputs are finite; a program needn't handle non-finite values.
Results may differ from the reference program's by a relative error of at most 0.0044.
Values may be sent and summed in bfloat16 or wider, within the bound.
No kernel may reach another device: no remote copies, remote signals or barrier semaphores. Data moves between devices by JAX's collectives and lax.ppermute only.
A program may use at most 128 MiB of HBM per device.

```python
import math
import jax
import jax.numpy as jnp
from jax import lax

EMBED = 256
VECS = 64
ITERS = 2
LM_DEV = 256
POOL_DEV = 2048
LANDMARKS = 4096
POOL = 32768


def draw_corpus(key, part):
    clusters = max(LANDMARKS // 16, 2)
    member = jax.random.randint(jax.random.fold_in(key, 11), (POOL,), 0, clusters)
    key_center = jax.random.fold_in(key, 12)
    key_basis = jax.random.fold_in(key, 13)
    key_coords = jax.random.fold_in(key, 14)
    key_noise = jax.random.fold_in(key, 15)
    center = 2.0 * jax.random.truncated_normal(key_center, -4.0, 4.0, (clusters, EMBED), jnp.float32)
    basis = 0.6 * jax.random.truncated_normal(key_basis, -4.0, 4.0, (4, clusters, EMBED), jnp.float32)
    coords = jax.random.truncated_normal(key_coords, -4.0, 4.0, (4, POOL, 1), jnp.float32)
    noise = 0.5 * jax.random.truncated_normal(key_noise, -4.0, 4.0, (POOL, EMBED), jnp.float32)
    rows_out = center[member] + noise
    for index in range(4):
        rows_out = rows_out + basis[index][member] * coords[index]
    return jnp.clip(rows_out, -20.0, 20.0)


def touch_ends(result, rng, smallest, largest):
    longest = result.shape.index(max(result.shape))
    spots = []
    for shift in (0, 1):
        where = [jax.random.randint(jax.random.fold_in(rng, axis), (), 0, length) for axis, length in enumerate(result.shape)]
        where[longest] = (where[longest] + shift) % result.shape[longest]
        spots.append(tuple(where))
    return result.at[spots[0]].set(smallest).at[spots[1]].set(largest)


def block_levels(rng, shape, cuts, smallest, largest):
    def one(dim, shards_of):
        heights = jax.random.uniform(jax.random.fold_in(jax.random.fold_in(rng, 6), dim), (shards_of,), jnp.float32, smallest / len(cuts), largest / len(cuts))
        return jnp.repeat(jnp.exp(heights), shape[dim] // shards_of).reshape((-1,) + (1,) * (len(shape) - dim - 1))

    loudness = one(*cuts[0])
    for cut in cuts[1:]:
        loudness = loudness * one(*cut)
    return loudness


def scatter_about(rng, dims, scale, bound, cuts=(), held_as=jnp.bfloat16):
    array = scale * jax.random.normal(rng, dims, jnp.float32)
    if cuts:
        array = array * block_levels(rng, dims, cuts, -0.22, 0.18)
    return jnp.clip(array, -bound, bound).astype(held_as)


def setup_inputs(seed: int = 0, part: int = 0) -> dict:
    keys = jax.random.split(jax.random.key(seed), 4)
    own_keys = jax.random.split(jax.random.fold_in(keys[3], part), 4)
    corpus = draw_corpus(jax.random.fold_in(jax.random.fold_in(keys[3], part), 71), part)
    sample_rows = touch_ends(jax.random.randint(own_keys[1], (LANDMARKS,), 0, POOL_DEV), jax.random.fold_in(own_keys[1], 1), 0, POOL_DEV - 1).astype(jnp.int32)
    initial = scatter_about(own_keys[2], (VECS, LANDMARKS), 1.0, 6.0, ((1, 16),), jnp.float32)
    return {"corpus": corpus, "sample_rows": sample_rows, "initial": initial}


def kernel_block(row_block, col_embeds, col_norms):
    embed_dim = row_block.shape[1]
    products = jnp.dot(row_block.astype(jnp.float32), col_embeds.astype(jnp.float32), precision=lax.Precision.HIGHEST, preferred_element_type=jnp.float32)
    row_norms = lax.optimization_barrier(jnp.sum(row_block * row_block, axis=1))
    distance = row_norms[:, None] + col_norms[None, :] - 2.0 * products
    return jnp.exp(-distance / (2.0 * embed_dim)).astype(jnp.bfloat16)

def reference(corpus, sample_rows, initial):
    landmark_ids = jnp.arange(LANDMARKS, dtype=jnp.int32) // LM_DEV * POOL_DEV + sample_rows.astype(jnp.int32)
    landmarks = corpus[landmark_ids]
    col_embeds = landmarks.T
    col_norms = lax.optimization_barrier(jnp.sum(col_embeds * col_embeds, axis=0))
    block_rows = math.gcd(LANDMARKS, 1024)
    blocks = landmarks.reshape(LANDMARKS // block_rows, block_rows, EMBED)
    landmark_count = float(LANDMARKS)
    vectors = initial - lax.optimization_barrier(jnp.sum(initial, axis=1, keepdims=True)) / landmark_count
    for sweep in range(ITERS):
        rounded = vectors.astype(jnp.bfloat16)

        def apply_block(row_block):
            kernel_rows = kernel_block(row_block, col_embeds, col_norms)
            return lax.dot_general(rounded.astype(jnp.float32), kernel_rows.astype(jnp.float32), (((1,), (1,)), ((), ())), preferred_element_type=jnp.float32)
        pieces = lax.map(apply_block, blocks)
        images = jnp.transpose(pieces, (1, 0, 2)).reshape(VECS, LANDMARKS)
        centered = images - lax.optimization_barrier(jnp.sum(images, axis=1, keepdims=True)) / landmark_count
        gram_matrix = jnp.dot(centered, centered.T, precision=lax.Precision.HIGHEST)
        factor = jnp.linalg.cholesky(gram_matrix)
        vectors = math.sqrt(landmark_count) * jax.scipy.linalg.solve_triangular(factor, centered, lower=True)
    return vectors
```

```python
import functools
import math

import jax
import jax.numpy as jnp
from jax import lax
from jax.experimental import pallas as pl
from jax.experimental.pallas import tpu as pltpu
from jax.sharding import PartitionSpec as P

ITERS = 2
REACH = 20.0
UNIT = REACH / 32767.0
FIXED = 2.0**28
HIGHEST = lax.Precision.HIGHEST
BF16, F32 = jnp.bfloat16, jnp.float32
VMEM = pl.BlockSpec(memory_space=pltpu.VMEM)


def matmul(a, b, contract, precision=None):
    return lax.dot_general(a, b, ((contract[:1], contract[1:]), ((), ())), precision=precision, preferred_element_type=F32)


def encode(landmarks, initial):
    half = landmarks.shape[0] // 2
    code = jnp.round(landmarks * (1.0 / UNIT)).astype(jnp.int32)
    packed = (code[:half] << 16) | (code[half:] & 0xFFFF)
    return jnp.concatenate([packed, jnp.round(initial * FIXED).astype(jnp.int32)], axis=0)


def split_codes(words):
    code = jnp.concatenate([words >> 16, (words << 16) >> 16], axis=0)
    high = ((code + 128) >> 8) << 8
    return high.astype(F32).astype(BF16), (code - high).astype(F32).astype(BF16)


def kernel_rows(words, own_high, own_low, own_norms, scale):
    high, low = split_codes(words)
    wide = high.astype(F32) + low.astype(F32)
    norms = scale * jnp.sum(wide * wide, axis=1, keepdims=True)
    dots = matmul(high, own_high, (1, 1)) + (matmul(high, own_low, (1, 1)) + matmul(low, own_high, (1, 1))) + matmul(low, own_low, (1, 1))
    return jnp.exp((2.0 * scale) * dots - (norms + own_norms)).astype(BF16)


def own_side(words, scale):
    high, low = split_codes(words)
    wide = high.astype(F32) + low.astype(F32)
    norms = matmul(jnp.ones((8, wide.shape[1]), F32), wide * wide, (1, 1), HIGHEST)[:1]
    return high, low, scale * norms


def build_kernel(count, half, scale, own_ref, *refs):
    blocks, out_ref = refs[:count], refs[count]
    own_high, own_low, own_norms = own_side(own_ref[:half], scale)
    for b, block in enumerate(blocks):
        out_ref[pl.ds(b * 2 * half, 2 * half), :] = kernel_rows(block[:half], own_high, own_low, own_norms, scale)


def first_kernel(count, last, half, scale, total, own_ref, *refs):
    blocks = refs[:count]
    parts = refs[count : count + (count // last) - 1]
    out_ref, tile_ref = refs[-2:]
    size = 2 * half
    own_high, own_low, own_norms = own_side(own_ref[:half], scale)
    for b, block in enumerate(blocks[count - last :]):
        tile_ref[pl.ds(b * size, size), :] = kernel_rows(block[:half], own_high, own_low, own_norms, scale)
    starts = [block[half:].astype(F32) * (1.0 / FIXED) for block in blocks]
    sums = starts[0]
    for start in starts[1:]:
        sums = sums + start
    mean = jnp.sum(sums, axis=1, keepdims=True) / total
    images = None
    for b, start in enumerate(starts):
        part, inner = divmod(b, last)
        ref = parts[part] if part < len(parts) else tile_ref
        term = matmul((start - mean).astype(BF16), ref[pl.ds(inner * size, size), :], (1, 0))
        images = term if images is None else images + term
    out_ref[...] = images


def inverse_factor(gram):
    n = gram.shape[0]
    row_id = lax.broadcasted_iota(jnp.int32, (n, 2 * n), 0)
    col_id = lax.broadcasted_iota(jnp.int32, (n, 2 * n), 1)
    eye = (row_id[:, :n] == col_id[:, :n]).astype(F32)
    work = jnp.concatenate([gram, eye], axis=1)
    done = []
    for top in range(0, n, 8):
        rows = n - top
        local = lax.broadcasted_iota(jnp.int32, (rows, 2 * n), 0)
        columns = [jnp.broadcast_to(work[:, top + k : top + k + 1], (rows, 2 * n)) for k in range(8)]
        for k in range(8):
            column = columns[k]
            factor = jnp.where(local > k, column * (1.0 / column[k : k + 1]), 0.0)
            work = work - factor * work[k : k + 1]
            for later in range(k + 1, 8):
                columns[later] = columns[later] - factor * columns[later][k : k + 1]
        done.append(work[:8])
        work = work[8:]
    upper = jnp.concatenate(done, axis=0)
    pivots = jnp.sum(jnp.where(row_id == col_id, upper, 0.0), axis=1, keepdims=True)
    return upper[:, n:] * lax.rsqrt(pivots)


def second_kernel(count, last, total, copies, *refs):
    images = refs[:count]
    tiles = refs[count : count + count // last]
    out_ref, share_ref = refs[-2:]
    size = images[0].shape[1]
    values = [image[...] for image in images]
    sums = values[0]
    for value in values[1:]:
        sums = sums + value
    mean = jnp.sum(sums, axis=1, keepdims=True) / total
    gram = None
    centered = []
    for value in values:
        centered.append(value - mean)
        term = matmul(centered[-1], centered[-1], (1, 1), HIGHEST)
        gram = term if gram is None else gram + term
    solve = math.sqrt(total) * inverse_factor(gram)
    result = None
    for b, value in enumerate(centered):
        part, inner = divmod(b, last)
        vectors = matmul(solve, value, (1, 0), HIGHEST).astype(BF16)
        term = matmul(vectors, tiles[part][pl.ds(inner * size, size), :], (1, 0))
        result = term if result is None else result + term
    out_ref[...] = result
    local_mean = jnp.sum(result, axis=1, keepdims=True) / size
    local = result - local_mean
    local_gram = matmul(local, local, (1, 1), HIGHEST)
    h = local_gram.shape[0] // 2
    share = jnp.concatenate(
        [local_gram[:h], local_gram[h:, h:], local_mean[:h], local_mean[h:], jnp.zeros((h, h - 2), F32)], axis=1
    )
    for c in range(copies):
        share_ref[c] = share


def last_kernel(total, shares_ref, images_ref, out_ref):
    copies, h, _ = shares_ref.shape
    size = images_ref.shape[1]
    shares = [shares_ref[c] for c in range(copies)]
    summed = shares[0]
    for share in shares[1:]:
        summed = summed + share
    means = jnp.concatenate([jnp.concatenate([s[:, 3 * h : 3 * h + 1], s[:, 3 * h + 1 : 3 * h + 2]], axis=0) for s in shares], axis=1)
    mean = jnp.sum(means, axis=1, keepdims=True) / copies
    apart = means - mean
    top = summed[:, : 2 * h]
    bottom = jnp.concatenate([top[:, h:].T, summed[:, 2 * h : 3 * h]], axis=1)
    gram = jnp.concatenate([top, bottom], axis=0) + size * matmul(apart, apart, (1, 1), HIGHEST)
    solve = math.sqrt(total) * inverse_factor(gram)
    out_ref[...] = matmul(solve, images_ref[...] - mean, (1, 0), HIGHEST)


def call(kernel, args, out_shape):
    return pl.pallas_call(
        kernel,
        out_shape=out_shape,
        in_specs=[VMEM] * len(args),
        out_specs=jax.tree.map(lambda _: VMEM, out_shape),
        compiler_params=pltpu.CompilerParams(vmem_limit_bytes=48 * 2**20),
    )(*args)


def gather_blocks(block):
    rows, cols = lax.axis_size("row"), lax.axis_size("col")

    def swap(value, axis, size, offset):
        return lax.ppermute(value, axis, [(i, i ^ offset) for i in range(size)]) if offset else value

    out = []
    for c in range(cols):
        along = swap(block, "col", cols, c)
        for r in range(0, rows, 2):
            chip = swap(along, "row", rows, r)
            out += [chip, swap(chip, "row", rows, 1)]
    return out


def local(corpus, sample_rows, initial):
    vecs, size = initial.shape
    half = size // 2
    rows, cols = lax.axis_size("row"), lax.axis_size("col")
    count = rows * cols
    last = rows
    total = float(size * count)
    scale = UNIT * UNIT / (2.0 * corpus.shape[1])
    landmarks = corpus.at[sample_rows].get(mode="promise_in_bounds")
    own = encode(landmarks, initial)
    blocks = gather_blocks(own)
    tiles = []
    for g in range(0, count - last, last):
        group = blocks[g : g + last]
        tiles.append(
            call(functools.partial(build_kernel, last, half, scale), [own] + group, jax.ShapeDtypeStruct((last * size, size), BF16))
        )
    images, tile = call(
        functools.partial(first_kernel, count, last, half, scale, total),
        [own] + blocks + tiles,
        (jax.ShapeDtypeStruct((vecs, size), F32), jax.ShapeDtypeStruct((last * size, size), BF16)),
    )
    tiles.append(tile)
    gathered = gather_blocks(images)
    images, share = call(
        functools.partial(second_kernel, count, last, total, count),
        gathered + tiles,
        (jax.ShapeDtypeStruct((vecs, size), F32), jax.ShapeDtypeStruct((count, vecs // 2, 2 * vecs), F32)),
    )
    shares = lax.all_to_all(share, ("row", "col"), split_axis=0, concat_axis=0)
    return call(functools.partial(last_kernel, total), [shares, images], jax.ShapeDtypeStruct((vecs, size), F32))


def local_large(corpus, sample_rows, initial):
    both = ("row", "col")
    landmarks = corpus[sample_rows]
    everyone = lax.all_gather(landmarks, both, axis=0, tiled=True)
    total = float(everyone.shape[0])
    norms = jnp.sum(everyone * everyone, axis=1)
    own_norms = jnp.sum(landmarks * landmarks, axis=1)
    products = jnp.dot(everyone, landmarks.T, precision=HIGHEST, preferred_element_type=F32)
    tile = jnp.exp(-(norms[:, None] + own_norms[None, :] - 2.0 * products) / (2.0 * corpus.shape[1])).astype(BF16)
    starts = lax.all_gather(initial, both, axis=1, tiled=True)
    rounded = (starts - jnp.mean(starts, axis=1, keepdims=True)).astype(BF16)
    vectors = None
    for _ in range(ITERS):
        images = jnp.dot(rounded, tile, preferred_element_type=F32)
        gathered = lax.all_gather(images, both, axis=1, tiled=True)
        mean = jnp.mean(gathered, axis=1, keepdims=True)
        centered = gathered - mean
        factor = jnp.linalg.cholesky(jnp.dot(centered, centered.T, precision=HIGHEST))
        rounded = (math.sqrt(total) * jax.scipy.linalg.solve_triangular(factor, centered, lower=True)).astype(BF16)
        vectors = math.sqrt(total) * jax.scipy.linalg.solve_triangular(factor, images - mean, lower=True)
    return vectors


def solution(mesh):
    shape = mesh.shape
    whole = P(("groups", "row", "col"))
    return jax.shard_map(
        local if shape["row"] * shape["col"] <= 16 else local_large,
        mesh=mesh,
        in_specs=(P(("groups", "row", "col"), None), whole, P(None, ("groups", "row", "col"))),
        out_specs=P(None, ("groups", "row", "col")),
        check_vma=False,
    )
```

```python
import functools
import math

import jax
import jax.numpy as jnp
from jax import lax
from jax.experimental import pallas as pl
from jax.experimental.pallas import tpu as pltpu
from jax.sharding import PartitionSpec as P

ITERS = 2
REACH = 20.0
UNIT = REACH / 32767.0
FIXED = 2.0**28
HIGHEST = lax.Precision.HIGHEST
BF16, F32 = jnp.bfloat16, jnp.float32
VMEM = pl.BlockSpec(memory_space=pltpu.VMEM)


def matmul(a, b, contract, precision=None):
    return lax.dot_general(a, b, ((contract[:1], contract[1:]), ((), ())), precision=precision, preferred_element_type=F32)


def encode(landmarks, initial):
    half = landmarks.shape[0] // 2
    code = jnp.round(landmarks * (1.0 / UNIT)).astype(jnp.int32)
    packed = (code[:half] << 16) | (code[half:] & 0xFFFF)
    return jnp.concatenate([packed, jnp.round(initial * FIXED).astype(jnp.int32)], axis=0)


def split_codes(words):
    code = jnp.concatenate([words >> 16, (words << 16) >> 16], axis=0)
    high = ((code + 128) >> 8) << 8
    return high.astype(F32).astype(BF16), (code - high).astype(F32).astype(BF16)


def kernel_rows(words, own_high, own_low, own_norms, scale):
    high, low = split_codes(words)
    wide = high.astype(F32) + low.astype(F32)
    norms = scale * jnp.sum(wide * wide, axis=1, keepdims=True)
    dots = matmul(high, own_high, (1, 1)) + (matmul(high, own_low, (1, 1)) + matmul(low, own_high, (1, 1))) + matmul(low, own_low, (1, 1))
    return jnp.exp((2.0 * scale) * dots - (norms + own_norms)).astype(BF16)


def own_side(words, scale):
    high, low = split_codes(words)
    wide = high.astype(F32) + low.astype(F32)
    norms = matmul(jnp.ones((8, wide.shape[1]), F32), wide * wide, (1, 1), HIGHEST)[:1]
    return high, low, scale * norms


def build_kernel(count, half, scale, own_ref, *refs):
    blocks, out_ref = refs[:count], refs[count]
    own_high, own_low, own_norms = own_side(own_ref[:half], scale)
    for b, block in enumerate(blocks):
        out_ref[pl.ds(b * 2 * half, 2 * half), :] = kernel_rows(block[:half], own_high, own_low, own_norms, scale)


def first_kernel(count, last, half, scale, total, own_ref, *refs):
    blocks = refs[:count]
    parts = refs[count : count + (count // last) - 1]
    out_ref, tile_ref = refs[-2:]
    size = 2 * half
    own_high, own_low, own_norms = own_side(own_ref[:half], scale)
    for b, block in enumerate(blocks[count - last :]):
        tile_ref[pl.ds(b * size, size), :] = kernel_rows(block[:half], own_high, own_low, own_norms, scale)
    starts = [block[half:].astype(F32) * (1.0 / FIXED) for block in blocks]
    sums = starts[0]
    for start in starts[1:]:
        sums = sums + start
    mean = jnp.sum(sums, axis=1, keepdims=True) / total
    images = None
    for b, start in enumerate(starts):
        part, inner = divmod(b, last)
        ref = parts[part] if part < len(parts) else tile_ref
        term = matmul((start - mean).astype(BF16), ref[pl.ds(inner * size, size), :], (1, 0))
        images = term if images is None else images + term
    out_ref[...] = images


def inverse_factor(gram):
    n = gram.shape[0]
    row_id = lax.broadcasted_iota(jnp.int32, (n, 2 * n), 0)
    col_id = lax.broadcasted_iota(jnp.int32, (n, 2 * n), 1)
    eye = (row_id[:, :n] == col_id[:, :n]).astype(F32)
    work = jnp.concatenate([gram, eye], axis=1)
    done = []
    for top in range(0, n, 8):
        rows = n - top
        local = lax.broadcasted_iota(jnp.int32, (rows, 2 * n), 0)
        columns = [jnp.broadcast_to(work[:, top + k : top + k + 1], (rows, 2 * n)) for k in range(8)]
        for k in range(8):
            column = columns[k]
            factor = jnp.where(local > k, column * (1.0 / column[k : k + 1]), 0.0)
            work = work - factor * work[k : k + 1]
            for later in range(k + 1, 8):
                columns[later] = columns[later] - factor * columns[later][k : k + 1]
        done.append(work[:8])
        work = work[8:]
    upper = jnp.concatenate(done, axis=0)
    pivots = jnp.sum(jnp.where(row_id == col_id, upper, 0.0), axis=1, keepdims=True)
    return upper[:, n:] * lax.rsqrt(pivots)


def thirds(value):
    high = value.astype(BF16)
    rest = value - high.astype(F32)
    middle = rest.astype(BF16)
    return jnp.concatenate([high, middle, (rest - middle.astype(F32)).astype(BF16)], axis=0)


def gram_of(stack):
    n = stack.shape[0] // 3
    p = matmul(stack, stack, (1, 1))
    middle = p[n : 2 * n, n : 2 * n] + (p[:n, 2 * n :] + p[2 * n :, :n])
    return p[:n, :n] + ((p[:n, n : 2 * n] + p[n : 2 * n, :n]) + middle)


def times(matrix, stack):
    n = matrix.shape[0]
    parts = thirds(matrix)
    p = matmul(jnp.concatenate([parts, parts, parts], axis=1), stack, (1, 0))
    return p[:n] + (p[n : 2 * n] + p[2 * n :])


def second_kernel(count, last, total, copies, *refs):
    images = refs[:count]
    tiles = refs[count : count + count // last]
    out_ref, share_ref = refs[-2:]
    size = images[0].shape[1]
    values = [image[...] for image in images]
    sums = values[0]
    for value in values[1:]:
        sums = sums + value
    mean = jnp.sum(sums, axis=1, keepdims=True) / total
    stack = thirds(jnp.concatenate([value - mean for value in values], axis=1))
    solve = math.sqrt(total) * inverse_factor(gram_of(stack))
    vectors = times(solve, stack).astype(BF16)
    result = None
    for t, tile in enumerate(tiles):
        depth = tile.shape[0]
        term = matmul(vectors[:, t * depth : (t + 1) * depth], tile[...], (1, 0))
        result = term if result is None else result + term
    out_ref[...] = result
    local_mean = jnp.sum(result, axis=1, keepdims=True) / size
    local_gram = gram_of(thirds(result - local_mean))
    h = local_gram.shape[0] // 2
    share = jnp.concatenate(
        [local_gram[:h], local_gram[h:, h:], local_mean[:h], local_mean[h:], jnp.zeros((h, h - 2), F32)], axis=1
    )
    for c in range(copies):
        share_ref[c] = share


def last_kernel(total, shares_ref, images_ref, out_ref):
    copies, h, _ = shares_ref.shape
    size = images_ref.shape[1]
    shares = [shares_ref[c] for c in range(copies)]
    summed = shares[0]
    for share in shares[1:]:
        summed = summed + share
    means = jnp.concatenate([jnp.concatenate([s[:, 3 * h : 3 * h + 1], s[:, 3 * h + 1 : 3 * h + 2]], axis=0) for s in shares], axis=1)
    mean = jnp.sum(means, axis=1, keepdims=True) / copies
    apart = means - mean
    top = summed[:, : 2 * h]
    bottom = jnp.concatenate([top[:, h:].T, summed[:, 2 * h : 3 * h]], axis=1)
    gram = jnp.concatenate([top, bottom], axis=0) + size * matmul(apart, apart, (1, 1), HIGHEST)
    solve = math.sqrt(total) * inverse_factor(gram)
    out_ref[...] = matmul(solve, images_ref[...] - mean, (1, 0), HIGHEST)


def call(kernel, args, out_shape, flops=0):
    return pl.pallas_call(
        kernel,
        out_shape=out_shape,
        in_specs=[VMEM] * len(args),
        out_specs=jax.tree.map(lambda _: VMEM, out_shape),
        compiler_params=pltpu.CompilerParams(vmem_limit_bytes=48 * 2**20),
        cost_estimate=pl.CostEstimate(flops=flops, bytes_accessed=flops // 300, transcendentals=0) if flops else None,
    )(*args)


def after(value, *others):
    return lax.optimization_barrier((value, *others))[0]


def gather_blocks(block, work=None):
    rows, cols = lax.axis_size("row"), lax.axis_size("col")

    def swap(value, axis, size, offset):
        return lax.ppermute(value, axis, [(i, i ^ offset) for i in range(size)])

    along = [block] + [swap(block, "col", cols, c) for c in range(1, cols)]
    groups, done = [], []
    for c in range(cols):
        chips = [along[c]]
        chips += [swap(along[c], "row", rows, r) for r in range(2, rows, 2)]
        if work and 1 <= c < cols:
            done.append(work(groups[c - 1]))
        if work and c == cols - 1:
            chips[-1] = after(chips[-1], *done[:-1])
        groups.append([b for chip in chips for b in (chip, swap(chip, "row", rows, 1))])
    return groups, done


def local(corpus, sample_rows, initial):
    vecs, size = initial.shape
    half = size // 2
    rows, cols = lax.axis_size("row"), lax.axis_size("col")
    count = rows * cols
    last = rows
    total = float(size * count)
    scale = UNIT * UNIT / (2.0 * corpus.shape[1])
    landmarks = lax.gather(
        corpus,
        sample_rows[:, None],
        lax.GatherDimensionNumbers(offset_dims=(1,), collapsed_slice_dims=(0,), start_index_map=(0,)),
        (1, corpus.shape[1]),
        mode="promise_in_bounds",
    )
    own = encode(landmarks, initial)

    def build(group):
        return call(functools.partial(build_kernel, last, half, scale), [own] + group, jax.ShapeDtypeStruct((last * size, size), BF16), 10**9)

    groups, tiles = gather_blocks(own, build)
    blocks = [block for group in groups for block in group]
    images, tile = call(
        functools.partial(first_kernel, count, last, half, scale, total),
        [own] + blocks + tiles,
        (jax.ShapeDtypeStruct((vecs, size), F32), jax.ShapeDtypeStruct((last * size, size), BF16)),
    )
    tiles.append(tile)
    gathered = [block for group in gather_blocks(images)[0] for block in group]
    images, share = call(
        functools.partial(second_kernel, count, last, total, count),
        gathered + tiles,
        (jax.ShapeDtypeStruct((vecs, size), F32), jax.ShapeDtypeStruct((count, vecs // 2, 2 * vecs), F32)),
    )
    shares = lax.all_to_all(share, ("row", "col"), split_axis=0, concat_axis=0)
    return call(functools.partial(last_kernel, total), [shares, images], jax.ShapeDtypeStruct((vecs, size), F32))


def local_large(corpus, sample_rows, initial):
    both = ("row", "col")
    landmarks = corpus[sample_rows]
    everyone = lax.all_gather(landmarks, both, axis=0, tiled=True)
    total = float(everyone.shape[0])
    norms = jnp.sum(everyone * everyone, axis=1)
    own_norms = jnp.sum(landmarks * landmarks, axis=1)
    products = jnp.dot(everyone, landmarks.T, precision=HIGHEST, preferred_element_type=F32)
    tile = jnp.exp(-(norms[:, None] + own_norms[None, :] - 2.0 * products) / (2.0 * corpus.shape[1])).astype(BF16)
    starts = lax.all_gather(initial, both, axis=1, tiled=True)
    rounded = (starts - jnp.mean(starts, axis=1, keepdims=True)).astype(BF16)
    vectors = None
    for _ in range(ITERS):
        images = jnp.dot(rounded, tile, preferred_element_type=F32)
        gathered = lax.all_gather(images, both, axis=1, tiled=True)
        mean = jnp.mean(gathered, axis=1, keepdims=True)
        centered = gathered - mean
        factor = jnp.linalg.cholesky(jnp.dot(centered, centered.T, precision=HIGHEST))
        rounded = (math.sqrt(total) * jax.scipy.linalg.solve_triangular(factor, centered, lower=True)).astype(BF16)
        vectors = math.sqrt(total) * jax.scipy.linalg.solve_triangular(factor, images - mean, lower=True)
    return vectors


def solution(mesh):
    shape = mesh.shape
    whole = P(("groups", "row", "col"))
    return jax.shard_map(
        local if shape["row"] * shape["col"] <= 16 else local_large,
        mesh=mesh,
        in_specs=(P(("groups", "row", "col"), None), whole, P(None, ("groups", "row", "col"))),
        out_specs=P(None, ("groups", "row", "col")),
        check_vma=False,
    )
```

```python
import functools
import math

import jax
import jax.numpy as jnp
from jax import lax
from jax.experimental import pallas as pl
from jax.experimental.pallas import tpu as pltpu
from jax.sharding import PartitionSpec as P

ITERS = 2
REACH = 20.0
UNIT = REACH / 32767.0
FIXED = 2.0**28
HIGHEST = lax.Precision.HIGHEST
BF16, F32 = jnp.bfloat16, jnp.float32
VMEM = pl.BlockSpec(memory_space=pltpu.VMEM)


def matmul(a, b, contract, precision=None):
    return lax.dot_general(a, b, ((contract[:1], contract[1:]), ((), ())), precision=precision, preferred_element_type=F32)


def encode(landmarks, initial):
    half = landmarks.shape[0] // 2
    code = jnp.round(landmarks * (1.0 / UNIT)).astype(jnp.int32)
    packed = (code[:half] << 16) | (code[half:] & 0xFFFF)
    return jnp.concatenate([packed, jnp.round(initial * FIXED).astype(jnp.int32)], axis=0)


def split_codes(words):
    code = jnp.concatenate([words >> 16, (words << 16) >> 16], axis=0)
    high = ((code + 128) >> 8) << 8
    return high.astype(F32).astype(BF16), (code - high).astype(F32).astype(BF16)


def kernel_rows(words, own_high, own_low, own_norms, scale):
    high, low = split_codes(words)
    wide = high.astype(F32) + low.astype(F32)
    norms = scale * jnp.sum(wide * wide, axis=1, keepdims=True)
    dots = matmul(high, own_high, (1, 1)) + (matmul(high, own_low, (1, 1)) + matmul(low, own_high, (1, 1))) + matmul(low, own_low, (1, 1))
    return jnp.exp((2.0 * scale) * dots - (norms + own_norms)).astype(BF16)


def own_side(refs, half, scale):
    parts = [split_codes(ref[:half]) for ref in refs]
    high = jnp.concatenate([part[0] for part in parts], axis=0)
    low = jnp.concatenate([part[1] for part in parts], axis=0)
    wide = high.astype(F32) + low.astype(F32)
    norms = matmul(jnp.ones((8, wide.shape[1]), F32), wide * wide, (1, 1), HIGHEST)[:1]
    return high, low, scale * norms


def build_kernel(half, scale, *refs):
    own, blocks, out_ref = refs[:2], refs[2:-1], refs[-1]
    own_high, own_low, own_norms = own_side(own, half, scale)
    for b, block in enumerate(blocks):
        out_ref[pl.ds(b * 2 * half, 2 * half), :] = kernel_rows(block[:half], own_high, own_low, own_norms, scale)


def first_kernel(counts, half, scale, total, *refs):
    count = sum(counts)
    own, blocks, parts = refs[:2], refs[2 : 2 + count], refs[2 + count : -2]
    out_ref, tile_ref = refs[-2:]
    size = 2 * half
    own_high, own_low, own_norms = own_side(own, half, scale)
    for b, block in enumerate(blocks[count - counts[-1] :]):
        tile_ref[pl.ds(b * size, size), :] = kernel_rows(block[:half], own_high, own_low, own_norms, scale)
    starts = [block[half:].astype(F32) * (1.0 / FIXED) for block in blocks]
    sums = starts[0]
    for start in starts[1:]:
        sums = sums + start
    mean = jnp.sum(sums, axis=1, keepdims=True) / total
    rounded = [(start - mean).astype(BF16) for start in starts]
    images = None
    for tile in (*parts, tile_ref):
        group, rounded = rounded[: tile.shape[0] // size], rounded[tile.shape[0] // size :]
        term = matmul(jnp.concatenate(group, axis=1), tile[...], (1, 0))
        images = term if images is None else images + term
    out_ref[...] = images


def inverse_factor(gram):
    n = gram.shape[0]
    row_id = lax.broadcasted_iota(jnp.int32, (n, 2 * n), 0)
    col_id = lax.broadcasted_iota(jnp.int32, (n, 2 * n), 1)
    eye = (row_id[:, :n] == col_id[:, :n]).astype(F32)
    work = jnp.concatenate([gram, eye], axis=1)
    done = []
    for top in range(0, n, 8):
        rows = n - top
        local = lax.broadcasted_iota(jnp.int32, (rows, 2 * n), 0)
        columns = [jnp.broadcast_to(work[:, top + k : top + k + 1], (rows, 2 * n)) for k in range(8)]
        for k in range(8):
            column = columns[k]
            factor = jnp.where(local > k, column * (1.0 / column[k : k + 1]), 0.0)
            work = work - factor * work[k : k + 1]
            for later in range(k + 1, 8):
                columns[later] = columns[later] - factor * columns[later][k : k + 1]
        done.append(work[:8])
        work = work[8:]
    upper = jnp.concatenate(done, axis=0)
    pivots = jnp.sum(jnp.where(row_id == col_id, upper, 0.0), axis=1, keepdims=True)
    return upper[:, n:] * lax.rsqrt(pivots)


def thirds(value):
    high = value.astype(BF16)
    rest = value - high.astype(F32)
    middle = rest.astype(BF16)
    return jnp.concatenate([high, middle, (rest - middle.astype(F32)).astype(BF16)], axis=0)


def gram_of(stack):
    n = stack.shape[0] // 3
    p = matmul(stack, stack, (1, 1))
    middle = p[n : 2 * n, n : 2 * n] + (p[:n, 2 * n :] + p[2 * n :, :n])
    return p[:n, :n] + ((p[:n, n : 2 * n] + p[n : 2 * n, :n]) + middle)


def times(matrix, stack):
    n = matrix.shape[0]
    parts = thirds(matrix)
    p = matmul(jnp.concatenate([parts, parts, parts], axis=1), stack, (1, 0))
    return p[:n] + (p[n : 2 * n] + p[2 * n :])


def second_kernel(pieces, total, *refs):
    count = 1 + max(piece[0] for piece in pieces)
    images, tiles = refs[:count], refs[count:-3]
    own_ref, other_ref, share_ref = refs[-3:]
    size = own_ref.shape[1]
    values = [images[i][:, b * size : (b + 1) * size] for i, b in pieces]
    sums = values[0]
    for value in values[1:]:
        sums = sums + value
    mean = jnp.sum(sums, axis=1, keepdims=True) / total
    stack = thirds(jnp.concatenate([value - mean for value in values], axis=1))
    solve = math.sqrt(total) * inverse_factor(gram_of(stack))
    vectors = times(solve, stack).astype(BF16)
    result, begin = None, 0
    for tile in tiles:
        end = begin + tile.shape[0]
        term = matmul(vectors[:, begin:end], tile[...], (1, 0))
        result, begin = term if result is None else result + term, end
    own_ref[...] = result[:, :size]
    other_ref[...] = result[:, size:]
    local_mean = jnp.sum(result, axis=1, keepdims=True) / (2 * size)
    gram = gram_of(thirds(result - local_mean))
    n = gram.shape[0]
    h = n // 2
    eye = lax.broadcasted_iota(jnp.int32, (n, n), 0) == lax.broadcasted_iota(jnp.int32, (n, n), 1)
    across = jnp.sum(jnp.where(eye, local_mean, 0.0), axis=0, keepdims=True)
    share_ref[:h] = jnp.concatenate([gram[:h], gram[h:, h:], local_mean[:h], local_mean[h:], jnp.zeros((h, h - 2), F32)], axis=1)
    share_ref[h:] = jnp.broadcast_to(jnp.concatenate([across, across[:, h:], jnp.zeros((1, h), F32)], axis=1), (8, 4 * h))


def merge(a, b, each):
    h = a.shape[0] - 8
    apart = a - b
    lane = lax.broadcasted_iota(jnp.int32, (h, 4 * h), 1)
    down = jnp.where(lane < 2 * h, apart[:h, 3 * h : 3 * h + 1], apart[:h, 3 * h + 1 : 3 * h + 2])
    both = a + b
    top = jnp.where(lane < 3 * h, both[:h] + (0.5 * each) * (down * apart[h : h + 1]), 0.5 * both[:h])
    return jnp.concatenate([top, 0.5 * both[h:]], axis=0)


def merge_kernel(each, a_ref, b_ref, out_ref):
    out_ref[...] = merge(a_ref[...], b_ref[...], each)


def last_kernel(total, outer_ref, share_ref, near_ref, far_ref, across_ref, own_ref, given_ref, out_ref):
    outer = outer_ref[0] == 1
    first = jnp.where(outer, near_ref[...], share_ref[...])
    second = jnp.where(outer, far_ref[...], across_ref[...])
    images = jnp.where(outer, given_ref[...], own_ref[...])
    share = merge(first, second, 0.5 * total)
    h = share.shape[0] - 8
    mean = jnp.concatenate([share[:h, 3 * h : 3 * h + 1], share[:h, 3 * h + 1 : 3 * h + 2]], axis=0)
    top = share[:h, : 2 * h]
    bottom = jnp.concatenate([top[:, h:].T, share[:h, 2 * h : 3 * h]], axis=1)
    solve = math.sqrt(total) * inverse_factor(jnp.concatenate([top, bottom], axis=0))
    out_ref[...] = times(solve, thirds(images - mean))


def call(kernel, args, out_shape, in_specs=None):
    return pl.pallas_call(
        kernel,
        out_shape=out_shape,
        in_specs=in_specs or [VMEM] * len(args),
        out_specs=jax.tree.map(lambda _: VMEM, out_shape),
        compiler_params=pltpu.CompilerParams(vmem_limit_bytes=24 * 2**20),
    )(*args)


def after(value, *others):
    return lax.optimization_barrier((value, *others))[0]


def exchange(axis, offset, size=4):
    return lambda value: lax.ppermute(value, axis, [(i, i ^ offset) for i in range(size)])


CORE, CHIP = exchange("row", 1), exchange("row", 2)
NEAR, FAR, OPPOSITE = exchange("col", 1), exchange("col", 2), exchange("col", 3)


def middle(value):
    return lax.ppermute(value, "col", MIDDLE)


MIDDLE = [(1, 2), (2, 1)]


def local(corpus, sample_rows, initial):
    vecs, size = initial.shape
    half = size // 2
    count = 16
    total = float(size * count)
    scale = UNIT * UNIT / (2.0 * corpus.shape[1])
    landmarks = lax.gather(
        corpus,
        sample_rows[:, None],
        lax.GatherDimensionNumbers(offset_dims=(1,), collapsed_slice_dims=(0,), start_index_map=(0,)),
        (1, corpus.shape[1]),
        mode="promise_in_bounds",
    )
    own = encode(landmarks, initial)

    def build(*blocks):
        shape = jax.ShapeDtypeStruct((len(blocks) * size, 2 * size), BF16)
        return call(functools.partial(build_kernel, half, scale), [own, outer, *blocks], shape)

    outer, partner, chip = NEAR(own), middle(own), CHIP(own)
    groups = [[own, outer, CORE(own), CORE(outer)]]
    tiles = [build(*groups[0])]
    partner_outer, chip_outer, chip_partner = middle(outer), NEAR(chip), CHIP(partner)
    groups.append([partner, CORE(partner), chip, CORE(chip)])
    tiles.append(build(*groups[1]))
    chip_partner_outer = CHIP(after(partner_outer, tiles[0]))
    groups.append([partner_outer, CORE(partner_outer), chip_outer, CORE(chip_outer)])
    tiles.append(build(*groups[2]))
    groups.append([chip_partner, CORE(chip_partner)])
    tiles.append(build(*groups[3]))
    groups.append([chip_partner_outer, CORE(after(chip_partner_outer, *tiles[1:4]))])
    images, tile = call(
        functools.partial(first_kernel, [len(group) for group in groups], half, scale, total),
        [own, outer] + [block for group in groups for block in group] + tiles,
        (jax.ShapeDtypeStruct((vecs, 2 * size), F32), jax.ShapeDtypeStruct((2 * size, 2 * size), BF16)),
    )
    tiles.append(tile)
    there, beside = middle(images), CHIP(images)
    beyond = CHIP(there)
    gathered = [images, there, beside, beyond]
    gathered += [CORE(value) for value in gathered]
    here, part, chip, far = 0, 1, 2, 3
    pieces = [(here, 0), (here, 1), (here + 4, 0), (here + 4, 1), (part, 0), (part + 4, 0), (chip, 0), (chip + 4, 0)]
    pieces += [(part, 1), (part + 4, 1), (chip, 1), (chip + 4, 1), (far, 0), (far + 4, 0), (far, 1), (far + 4, 1)]
    block = jax.ShapeDtypeStruct((vecs, size), F32)
    packed = jax.ShapeDtypeStruct((vecs // 2 + 8, 2 * vecs), F32)
    images, other, share = call(functools.partial(second_kernel, pieces, total), gathered + tiles, (block, block, packed))
    given = NEAR(other)
    for step, swap in enumerate((CORE, CHIP)):
        share = call(functools.partial(merge_kernel, 2.0 * size * 2**step), [share, swap(share)], packed)
    place = lax.axis_index("col")
    flag = ((place == 0) | (place == 3)).astype(jnp.int32).reshape(1)
    return call(
        functools.partial(last_kernel, total),
        [flag, share, NEAR(share), FAR(share), OPPOSITE(share), images, given],
        block,
        [pl.BlockSpec(memory_space=pltpu.SMEM)] + [VMEM] * 6,
    )


def local_large(corpus, sample_rows, initial):
    both = ("row", "col")
    landmarks = corpus[sample_rows]
    everyone = lax.all_gather(landmarks, both, axis=0, tiled=True)
    total = float(everyone.shape[0])
    norms = jnp.sum(everyone * everyone, axis=1)
    own_norms = jnp.sum(landmarks * landmarks, axis=1)
    products = jnp.dot(everyone, landmarks.T, precision=HIGHEST, preferred_element_type=F32)
    tile = jnp.exp(-(norms[:, None] + own_norms[None, :] - 2.0 * products) / (2.0 * corpus.shape[1])).astype(BF16)
    starts = lax.all_gather(initial, both, axis=1, tiled=True)
    rounded = (starts - jnp.mean(starts, axis=1, keepdims=True)).astype(BF16)
    vectors = None
    for _ in range(ITERS):
        images = jnp.dot(rounded, tile, preferred_element_type=F32)
        gathered = lax.all_gather(images, both, axis=1, tiled=True)
        mean = jnp.mean(gathered, axis=1, keepdims=True)
        centered = gathered - mean
        factor = jnp.linalg.cholesky(jnp.dot(centered, centered.T, precision=HIGHEST))
        rounded = (math.sqrt(total) * jax.scipy.linalg.solve_triangular(factor, centered, lower=True)).astype(BF16)
        vectors = math.sqrt(total) * jax.scipy.linalg.solve_triangular(factor, images - mean, lower=True)
    return vectors


def solution(mesh):
    shape = mesh.shape
    whole = P(("groups", "row", "col"))
    return jax.shard_map(
        local if (shape["row"], shape["col"]) == (4, 4) else local_large,
        mesh=mesh,
        in_specs=(P(("groups", "row", "col"), None), whole, P(None, ("groups", "row", "col"))),
        out_specs=P(None, ("groups", "row", "col")),
        check_vma=False,
    )
```

```python
import functools
import math

import jax
import jax.numpy as jnp
from jax import lax
from jax.experimental import pallas as pl
from jax.experimental.pallas import tpu as pltpu
from jax.sharding import PartitionSpec as P

ITERS = 2
REACH = 20.0
UNIT = REACH / 32767.0
FIXED = 2.0**28
HIGHEST = lax.Precision.HIGHEST
BF16, F32 = jnp.bfloat16, jnp.float32
VMEM = pl.BlockSpec(memory_space=pltpu.VMEM)


def matmul(a, b, contract, precision=None):
    return lax.dot_general(a, b, ((contract[:1], contract[1:]), ((), ())), precision=precision, preferred_element_type=F32)


def encode(landmarks, initial):
    half = landmarks.shape[0] // 2
    code = jnp.round(landmarks * (1.0 / UNIT)).astype(jnp.int32)
    packed = (code[:half] << 16) | (code[half:] & 0xFFFF)
    return jnp.concatenate([packed, jnp.round(initial * FIXED).astype(jnp.int32)], axis=0)


def split_codes(words):
    code = jnp.concatenate([words >> 16, (words << 16) >> 16], axis=0)
    high = ((code + 128) >> 8) << 8
    return high.astype(F32).astype(BF16), (code - high).astype(F32).astype(BF16)


def kernel_rows(words, own_high, own_low, own_norms, scale):
    high, low = split_codes(words)
    wide = high.astype(F32) + low.astype(F32)
    norms = scale * jnp.sum(wide * wide, axis=1, keepdims=True)
    dots = matmul(high, own_high, (1, 1)) + (matmul(high, own_low, (1, 1)) + matmul(low, own_high, (1, 1))) + matmul(low, own_low, (1, 1))
    return jnp.exp((2.0 * scale) * dots - (norms + own_norms)).astype(BF16)


def own_side(refs, half, scale):
    parts = [split_codes(ref[:half]) for ref in refs]
    high = jnp.concatenate([part[0] for part in parts], axis=0)
    low = jnp.concatenate([part[1] for part in parts], axis=0)
    wide = high.astype(F32) + low.astype(F32)
    norms = matmul(jnp.ones((8, wide.shape[1]), F32), wide * wide, (1, 1), HIGHEST)[:1]
    return high, low, scale * norms


def build_kernel(half, scale, *refs):
    own, blocks, out_ref = refs[:2], refs[2:-1], refs[-1]
    own_high, own_low, own_norms = own_side(own, half, scale)
    for b, block in enumerate(blocks):
        out_ref[pl.ds(b * 2 * half, 2 * half), :] = kernel_rows(block[:half], own_high, own_low, own_norms, scale)


def first_kernel(counts, half, scale, total, *refs):
    count = sum(counts)
    own, blocks, parts = refs[:2], refs[2 : 2 + count], refs[2 + count : -2]
    out_ref, tile_ref = refs[-2:]
    size = 2 * half
    own_high, own_low, own_norms = own_side(own, half, scale)
    for b, block in enumerate(blocks[count - counts[-1] :]):
        tile_ref[pl.ds(b * size, size), :] = kernel_rows(block[:half], own_high, own_low, own_norms, scale)
    starts = [block[half:].astype(F32) * (1.0 / FIXED) for block in blocks]
    sums = starts[0]
    for start in starts[1:]:
        sums = sums + start
    mean = jnp.sum(sums, axis=1, keepdims=True) / total
    rounded = [(start - mean).astype(BF16) for start in starts]
    images = None
    for tile in (*parts, tile_ref):
        group, rounded = rounded[: tile.shape[0] // size], rounded[tile.shape[0] // size :]
        term = matmul(jnp.concatenate(group, axis=1), tile[...], (1, 0))
        images = term if images is None else images + term
    out_ref[...] = images


def inverse_factor(gram):
    n = gram.shape[0]
    row_id = lax.broadcasted_iota(jnp.int32, (n, 2 * n), 0)
    col_id = lax.broadcasted_iota(jnp.int32, (n, 2 * n), 1)
    eye = (row_id[:, :n] == col_id[:, :n]).astype(F32)
    work = jnp.concatenate([gram, eye], axis=1)
    done = []
    for top in range(0, n, 8):
        rows = n - top
        place = lax.broadcasted_iota(jnp.int32, (rows, 2 * n), 0)
        columns = [jnp.broadcast_to(work[:, top + k : top + k + 1], (rows, 2 * n)) for k in range(8)]
        for k in range(0, 8, 2):
            one, two = columns[k], columns[k + 1]
            a, b, d = one[k : k + 1], one[k + 1 : k + 2], two[k + 1 : k + 2]
            inverse = 1.0 / a
            slope = b * inverse
            second = jnp.where(place > k + 1, (two * a - one * b) * (1.0 / (a * d - b * b)), 0.0)
            first = jnp.where(place > k, one, 0.0)

            def eliminate(value):
                upper = value[k : k + 1]
                return value - first * (upper * inverse) - second * (value[k + 1 : k + 2] - slope * upper)

            work = eliminate(work)
            columns = columns[: k + 2] + [eliminate(column) for column in columns[k + 2 :]]
        done.append(work[:8])
        work = work[8:]
    upper = jnp.concatenate(done, axis=0)
    pivots = jnp.sum(jnp.where(row_id == col_id, upper, 0.0), axis=1, keepdims=True)
    return upper[:, n:] * lax.rsqrt(pivots)


def thirds(value):
    high = value.astype(BF16)
    rest = value - high.astype(F32)
    middle = rest.astype(BF16)
    return jnp.concatenate([high, middle, (rest - middle.astype(F32)).astype(BF16)], axis=0)


def gram_of(stack):
    n = stack.shape[0] // 3
    p = matmul(stack, stack, (1, 1))
    middle = p[n : 2 * n, n : 2 * n] + (p[:n, 2 * n :] + p[2 * n :, :n])
    return p[:n, :n] + ((p[:n, n : 2 * n] + p[n : 2 * n, :n]) + middle)


def times(matrix, stack):
    n = matrix.shape[0]
    parts = thirds(matrix)
    p = matmul(jnp.concatenate([parts, parts, parts], axis=1), stack, (1, 0))
    return p[:n] + (p[n : 2 * n] + p[2 * n :])


def second_kernel(pieces, total, *refs):
    count = 1 + max(piece[0] for piece in pieces)
    images, tiles = refs[:count], refs[count:-3]
    own_ref, other_ref, share_ref = refs[-3:]
    size = own_ref.shape[1]
    values = [images[i][:, b * size : (b + 1) * size] for i, b in pieces]
    sums = values[0]
    for value in values[1:]:
        sums = sums + value
    mean = jnp.sum(sums, axis=1, keepdims=True) / total
    stack = thirds(jnp.concatenate([value - mean for value in values], axis=1))
    solve = math.sqrt(total) * inverse_factor(gram_of(stack))
    vectors = times(solve, stack).astype(BF16)
    result, begin = None, 0
    for tile in tiles:
        end = begin + tile.shape[0]
        term = matmul(vectors[:, begin:end], tile[...], (1, 0))
        result, begin = term if result is None else result + term, end
    own_ref[...] = result[:, :size]
    other_ref[...] = result[:, size:]
    local_mean = jnp.sum(result, axis=1, keepdims=True) / (2 * size)
    gram = gram_of(thirds(result - local_mean))
    n = gram.shape[0]
    h = n // 2
    eye = lax.broadcasted_iota(jnp.int32, (n, n), 0) == lax.broadcasted_iota(jnp.int32, (n, n), 1)
    across = jnp.sum(jnp.where(eye, local_mean, 0.0), axis=0, keepdims=True)
    share_ref[:h] = jnp.concatenate([gram[:h], gram[h:, h:], local_mean[:h], local_mean[h:], jnp.zeros((h, h - 2), F32)], axis=1)
    share_ref[h:] = jnp.broadcast_to(jnp.concatenate([across, across[:, h:], jnp.zeros((1, h), F32)], axis=1), (8, 4 * h))


def merge(a, b, each):
    h = a.shape[0] - 8
    apart = a - b
    lane = lax.broadcasted_iota(jnp.int32, (h, 4 * h), 1)
    down = jnp.where(lane < 2 * h, apart[:h, 3 * h : 3 * h + 1], apart[:h, 3 * h + 1 : 3 * h + 2])
    both = a + b
    top = jnp.where(lane < 3 * h, both[:h] + (0.5 * each) * (down * apart[h : h + 1]), 0.5 * both[:h])
    return jnp.concatenate([top, 0.5 * both[h:]], axis=0)


def merge_kernel(each, a_ref, b_ref, out_ref):
    out_ref[...] = merge(a_ref[...], b_ref[...], each)


def last_kernel(total, outer_ref, share_ref, near_ref, far_ref, across_ref, own_ref, given_ref, out_ref):
    outer = outer_ref[0] == 1
    first = jnp.where(outer, near_ref[...], share_ref[...])
    second = jnp.where(outer, far_ref[...], across_ref[...])
    images = jnp.where(outer, given_ref[...], own_ref[...])
    share = merge(first, second, 0.5 * total)
    h = share.shape[0] - 8
    mean = jnp.concatenate([share[:h, 3 * h : 3 * h + 1], share[:h, 3 * h + 1 : 3 * h + 2]], axis=0)
    top = share[:h, : 2 * h]
    bottom = jnp.concatenate([top[:, h:].T, share[:h, 2 * h : 3 * h]], axis=1)
    solve = math.sqrt(total) * inverse_factor(jnp.concatenate([top, bottom], axis=0))
    out_ref[...] = times(solve, thirds(images - mean))


def call(kernel, args, out_shape, in_specs=None):
    return pl.pallas_call(
        kernel,
        out_shape=out_shape,
        in_specs=in_specs or [VMEM] * len(args),
        out_specs=jax.tree.map(lambda _: VMEM, out_shape),
        compiler_params=pltpu.CompilerParams(vmem_limit_bytes=24 * 2**20),
    )(*args)


def after(value, *others):
    return lax.optimization_barrier((value, *others))[0]


def exchange(axis, offset, size=4):
    return lambda value: lax.ppermute(value, axis, [(i, i ^ offset) for i in range(size)])


CORE, CHIP = exchange("row", 1), exchange("row", 2)
NEAR, FAR, OPPOSITE = exchange("col", 1), exchange("col", 2), exchange("col", 3)


def middle(value):
    return lax.ppermute(value, "col", MIDDLE)


def diagonal(value):
    return lax.ppermute(value, ("row", "col"), [(4 * r + c, 4 * (r ^ 2) + 3 - c) for r in range(4) for c in (1, 2)])


MIDDLE = [(1, 2), (2, 1)]


def local(corpus, sample_rows, initial):
    vecs, size = initial.shape
    half = size // 2
    count = 16
    total = float(size * count)
    scale = UNIT * UNIT / (2.0 * corpus.shape[1])
    landmarks = lax.gather(
        corpus,
        sample_rows[:, None],
        lax.GatherDimensionNumbers(offset_dims=(1,), collapsed_slice_dims=(0,), start_index_map=(0,)),
        (1, corpus.shape[1]),
        mode="promise_in_bounds",
    )
    own = encode(landmarks, initial)

    def build(*blocks):
        shape = jax.ShapeDtypeStruct((len(blocks) * size, 2 * size), BF16)
        return call(functools.partial(build_kernel, half, scale), [own, outer, *blocks], shape)

    outer, partner, chip = NEAR(own), middle(own), CHIP(own)
    groups = [[own, outer, CORE(own), CORE(outer)]]
    tiles = [build(*groups[0])]
    partner_outer, chip_outer, chip_partner = middle(outer), NEAR(chip), CHIP(partner)
    groups.append([partner, CORE(partner), chip, CORE(chip)])
    tiles.append(build(*groups[1]))
    chip_partner_outer = CHIP(after(partner_outer, tiles[0]))
    groups.append([partner_outer, CORE(partner_outer), chip_outer, CORE(chip_outer)])
    tiles.append(build(*groups[2]))
    groups.append([chip_partner, CORE(chip_partner)])
    tiles.append(build(*groups[3]))
    final = CORE(after(chip_partner_outer, *tiles[1:4]))
    groups.append([chip_partner_outer])
    tiles.append(build(*groups[4]))
    groups.append([final])
    images, tile = call(
        functools.partial(first_kernel, [len(group) for group in groups], half, scale, total),
        [own, outer] + [block for group in groups for block in group] + tiles,
        (jax.ShapeDtypeStruct((vecs, 2 * size), F32), jax.ShapeDtypeStruct((size, 2 * size), BF16)),
    )
    tiles.append(tile)
    there, beside = middle(images), CHIP(images)
    beyond = diagonal(images)
    gathered = [images, there, beside, beyond]
    gathered += [CORE(value) for value in gathered]
    here, part, chip, far = 0, 1, 2, 3
    pieces = [(here, 0), (here, 1), (here + 4, 0), (here + 4, 1), (part, 0), (part + 4, 0), (chip, 0), (chip + 4, 0)]
    pieces += [(part, 1), (part + 4, 1), (chip, 1), (chip + 4, 1), (far, 0), (far + 4, 0), (far, 1), (far + 4, 1)]
    block = jax.ShapeDtypeStruct((vecs, size), F32)
    packed = jax.ShapeDtypeStruct((vecs // 2 + 8, 2 * vecs), F32)
    images, other, share = call(functools.partial(second_kernel, pieces, total), gathered + tiles, (block, block, packed))
    given = NEAR(other)
    for step, swap in enumerate((CORE, CHIP)):
        share = call(functools.partial(merge_kernel, 2.0 * size * 2**step), [share, swap(share)], packed)
    place = lax.axis_index("col")
    flag = ((place == 0) | (place == 3)).astype(jnp.int32).reshape(1)
    return call(
        functools.partial(last_kernel, total),
        [flag, share, NEAR(share), FAR(share), OPPOSITE(share), images, given],
        block,
        [pl.BlockSpec(memory_space=pltpu.SMEM)] + [VMEM] * 6,
    )


def local_large(corpus, sample_rows, initial):
    both = ("row", "col")
    landmarks = corpus[sample_rows]
    everyone = lax.all_gather(landmarks, both, axis=0, tiled=True)
    total = float(everyone.shape[0])
    norms = jnp.sum(everyone * everyone, axis=1)
    own_norms = jnp.sum(landmarks * landmarks, axis=1)
    products = jnp.dot(everyone, landmarks.T, precision=HIGHEST, preferred_element_type=F32)
    tile = jnp.exp(-(norms[:, None] + own_norms[None, :] - 2.0 * products) / (2.0 * corpus.shape[1])).astype(BF16)
    starts = lax.all_gather(initial, both, axis=1, tiled=True)
    rounded = (starts - jnp.mean(starts, axis=1, keepdims=True)).astype(BF16)
    vectors = None
    for _ in range(ITERS):
        images = jnp.dot(rounded, tile, preferred_element_type=F32)
        gathered = lax.all_gather(images, both, axis=1, tiled=True)
        mean = jnp.mean(gathered, axis=1, keepdims=True)
        centered = gathered - mean
        factor = jnp.linalg.cholesky(jnp.dot(centered, centered.T, precision=HIGHEST))
        rounded = (math.sqrt(total) * jax.scipy.linalg.solve_triangular(factor, centered, lower=True)).astype(BF16)
        vectors = math.sqrt(total) * jax.scipy.linalg.solve_triangular(factor, images - mean, lower=True)
    return vectors


def solution(mesh):
    shape = mesh.shape
    whole = P(("groups", "row", "col"))
    return jax.shard_map(
        local if (shape["row"], shape["col"]) == (4, 4) else local_large,
        mesh=mesh,
        in_specs=(P(("groups", "row", "col"), None), whole, P(None, ("groups", "row", "col"))),
        out_specs=P(None, ("groups", "row", "col")),
        check_vma=False,
    )
```

```python
import functools
import math

import jax
import jax.numpy as jnp
from jax import lax
from jax.experimental import pallas as pl
from jax.experimental.pallas import tpu as pltpu
from jax.sharding import PartitionSpec as P

ITERS = 2
REACH = 20.0
UNIT = REACH / 32767.0
FIXED, RANGE = 2.0**28, 2.0**26
HIGHEST = lax.Precision.HIGHEST
BF16, F32 = jnp.bfloat16, jnp.float32
VMEM = pl.BlockSpec(memory_space=pltpu.VMEM)


def matmul(a, b, contract, precision=None):
    return lax.dot_general(a, b, ((contract[:1], contract[1:]), ((), ())), precision=precision, preferred_element_type=F32)


def pair(high, low):
    return (high << 16) | (low & 0xFFFF)


def unpair(words):
    return words >> 16, (words << 16) >> 16


def encode(initial_ref, out_ref):
    initial = initial_ref[...]
    vecs, size = initial.shape
    half = size // 2
    mean = jnp.round(jnp.sum(initial, axis=1, keepdims=True) * (FIXED / size)).astype(jnp.int32)
    apart = initial - mean.astype(F32) * (1.0 / FIXED)
    reach = jnp.ceil(jnp.max(jnp.abs(apart), axis=1, keepdims=True) * RANGE).astype(jnp.int32) + 1
    step = reach.astype(F32) * (1.0 / (RANGE * 32767.0))
    level = jnp.round(apart / step).astype(jnp.int32)
    words = pair(level[:, :half], level[:, half:])
    row = lax.broadcasted_iota(jnp.int32, (vecs, size), 0)
    lane = lax.broadcasted_iota(jnp.int32, (vecs, size), 1)
    header = jnp.where(lane == row, mean, jnp.where(lane == row + vecs, reach, 0))
    out_ref[: vecs // 2] = jnp.concatenate([words[: vecs // 2], words[vecs // 2 :]], axis=1)
    out_ref[vecs // 2 :] = jnp.broadcast_to(jnp.sum(header, axis=0, keepdims=True), (8, size))


def decode(block, half):
    words = block[half : block.shape[0] - 8]
    vecs = 2 * words.shape[0]
    level = jnp.concatenate([jnp.concatenate(unpair(part), axis=1) for part in (words[:, :half], words[:, half:])], axis=0)
    header = block[block.shape[0] - 8 :].astype(F32)[:1, : 2 * vecs]
    row = lax.broadcasted_iota(jnp.int32, (vecs, 2 * vecs), 0)
    lane = lax.broadcasted_iota(jnp.int32, (vecs, 2 * vecs), 1)
    mean = jnp.sum(jnp.where(lane == row, header, 0.0), axis=1, keepdims=True) * (1.0 / FIXED)
    step = jnp.sum(jnp.where(lane == row + vecs, header, 0.0), axis=1, keepdims=True) * (1.0 / (RANGE * 32767.0))
    return level.astype(F32) * step + mean


def split_codes(words):
    code = jnp.concatenate(unpair(words), axis=0)
    high = ((code + 128) >> 8) << 8
    return high.astype(F32).astype(BF16), (code - high).astype(F32).astype(BF16)


def kernel_rows(words, own_high, own_low, own_norms, scale):
    high, low = split_codes(words)
    wide = high.astype(F32) + low.astype(F32)
    norms = scale * jnp.sum(wide * wide, axis=1, keepdims=True)
    dots = matmul(high, own_high, (1, 1)) + (matmul(high, own_low, (1, 1)) + matmul(low, own_high, (1, 1))) + matmul(low, own_low, (1, 1))
    return jnp.exp((2.0 * scale) * dots - (norms + own_norms)).astype(BF16)


def own_side(refs, half, scale):
    parts = [split_codes(ref[:half]) for ref in refs]
    high = jnp.concatenate([part[0] for part in parts], axis=0)
    low = jnp.concatenate([part[1] for part in parts], axis=0)
    wide = high.astype(F32) + low.astype(F32)
    norms = matmul(jnp.ones((8, wide.shape[1]), F32), wide * wide, (1, 1), HIGHEST)[:1]
    return high, low, scale * norms


def side_kernel(half, scale, own_ref, outer_ref, high_ref, low_ref, norms_ref):
    high_ref[...], low_ref[...], norms_ref[...] = own_side((own_ref, outer_ref), half, scale)


def build_kernel(half, scale, *refs):
    side, blocks, (tile_ref, start_ref) = refs[:3], refs[3:-2], refs[-2:]
    for b, block in enumerate(blocks):
        place = pl.ds(b * 2 * half, 2 * half)
        tile_ref[place, :] = kernel_rows(block[:half], *(ref[...] for ref in side), scale)
        start_ref[:, place] = decode(block[...], half)


def first_kernel(count, half, scale, total, *refs):
    side, block, tiles, parts = refs[:3], refs[3], refs[4 : 4 + count], refs[4 + count : -2]
    out_ref, tile_ref = refs[-2:]
    size = 2 * half
    tile_ref[...] = kernel_rows(block[:half], *(ref[...] for ref in side), scale)
    starts = [part[...] for part in parts] + [decode(block[...], half)]
    pieces = [start[:, b : b + size] for start in starts for b in range(0, start.shape[1], size)]
    sums = pieces[0]
    for piece in pieces[1:]:
        sums = sums + piece
    mean = jnp.sum(sums, axis=1, keepdims=True) / total
    images = None
    for start, tile in zip(starts, (*tiles, tile_ref)):
        term = matmul((start - mean).astype(BF16), tile[...], (1, 0))
        images = term if images is None else images + term
    out_ref[...] = images


def inverse_factor(gram):
    n = gram.shape[0]
    row_id = lax.broadcasted_iota(jnp.int32, (n, 2 * n), 0)
    col_id = lax.broadcasted_iota(jnp.int32, (n, 2 * n), 1)
    eye = (row_id[:, :n] == col_id[:, :n]).astype(F32)
    work = jnp.concatenate([gram, eye], axis=1)
    done = []
    for top in range(0, n, 8):
        rows = n - top
        place = lax.broadcasted_iota(jnp.int32, (rows, 2 * n), 0)
        columns = [jnp.broadcast_to(work[:, top + k : top + k + 1], (rows, 2 * n)) for k in range(8)]
        for k in range(0, 8, 2):
            one, two = columns[k], columns[k + 1]
            a, b, d = one[k : k + 1], one[k + 1 : k + 2], two[k + 1 : k + 2]
            inverse = 1.0 / a
            slope = b * inverse
            second = jnp.where(place > k + 1, (two * a - one * b) * (1.0 / (a * d - b * b)), 0.0)
            first = jnp.where(place > k, one, 0.0)

            def eliminate(value):
                upper = value[k : k + 1]
                return value - first * (upper * inverse) - second * (value[k + 1 : k + 2] - slope * upper)

            work = eliminate(work)
            columns = columns[: k + 2] + [eliminate(column) for column in columns[k + 2 :]]
        done.append(work[:8])
        work = work[8:]
    upper = jnp.concatenate(done, axis=0)
    pivots = jnp.sum(jnp.where(row_id == col_id, upper, 0.0), axis=1, keepdims=True)
    return upper[:, n:] * lax.rsqrt(pivots)


def thirds(value):
    high = value.astype(BF16)
    rest = value - high.astype(F32)
    middle = rest.astype(BF16)
    return jnp.concatenate([high, middle, (rest - middle.astype(F32)).astype(BF16)], axis=0)


def gram_of(stack):
    n = stack.shape[0] // 3
    p = matmul(stack, stack, (1, 1))
    middle = p[n : 2 * n, n : 2 * n] + (p[:n, 2 * n :] + p[2 * n :, :n])
    return p[:n, :n] + ((p[:n, n : 2 * n] + p[n : 2 * n, :n]) + middle)


def times(matrix, stack):
    n = matrix.shape[0]
    parts = thirds(matrix)
    p = matmul(jnp.concatenate([parts, parts, parts], axis=1), stack, (1, 0))
    return p[:n] + (p[n : 2 * n] + p[2 * n :])


def second_kernel(pieces, total, *refs):
    count = 1 + max(piece[0] for piece in pieces)
    images, tiles = refs[:count], refs[count:-3]
    own_ref, other_ref, share_ref = refs[-3:]
    size = own_ref.shape[1]
    values = [images[i][:, b * size : (b + 1) * size] for i, b in pieces]
    sums = values[0]
    for value in values[1:]:
        sums = sums + value
    mean = jnp.sum(sums, axis=1, keepdims=True) / total
    stack = thirds(jnp.concatenate([value - mean for value in values], axis=1))
    solve = math.sqrt(total) * inverse_factor(gram_of(stack))
    vectors = times(solve, stack).astype(BF16)
    result, begin = None, 0
    for tile in tiles:
        end = begin + tile.shape[0]
        term = matmul(vectors[:, begin:end], tile[...], (1, 0))
        result, begin = term if result is None else result + term, end
    own_ref[...] = result[:, :size]
    other_ref[...] = result[:, size:]
    local_mean = jnp.sum(result, axis=1, keepdims=True) / (2 * size)
    gram = gram_of(thirds(result - local_mean))
    n = gram.shape[0]
    h = n // 2
    eye = lax.broadcasted_iota(jnp.int32, (n, n), 0) == lax.broadcasted_iota(jnp.int32, (n, n), 1)
    across = jnp.sum(jnp.where(eye, local_mean, 0.0), axis=0, keepdims=True)
    share_ref[:h] = jnp.concatenate([gram[:h], gram[h:, h:], local_mean[:h], local_mean[h:], jnp.zeros((h, h - 2), F32)], axis=1)
    share_ref[h:] = jnp.broadcast_to(jnp.concatenate([across, across[:, h:], jnp.zeros((1, h), F32)], axis=1), (8, 4 * h))


def merge(a, b, each):
    h = a.shape[0] - 8
    apart = a - b
    lane = lax.broadcasted_iota(jnp.int32, (h, 4 * h), 1)
    down = jnp.where(lane < 2 * h, apart[:h, 3 * h : 3 * h + 1], apart[:h, 3 * h + 1 : 3 * h + 2])
    both = a + b
    top = jnp.where(lane < 3 * h, both[:h] + (0.5 * each) * (down * apart[h : h + 1]), 0.5 * both[:h])
    return jnp.concatenate([top, 0.5 * both[h:]], axis=0)


def merge_kernel(each, a_ref, b_ref, out_ref):
    out_ref[...] = merge(a_ref[...], b_ref[...], each)


def last_kernel(total, outer_ref, share_ref, near_ref, far_ref, across_ref, own_ref, given_ref, out_ref):
    outer = outer_ref[0] == 1
    first = jnp.where(outer, near_ref[...], share_ref[...])
    second = jnp.where(outer, far_ref[...], across_ref[...])
    images = jnp.where(outer, given_ref[...], own_ref[...])
    share = merge(first, second, 0.5 * total)
    h = share.shape[0] - 8
    mean = jnp.concatenate([share[:h, 3 * h : 3 * h + 1], share[:h, 3 * h + 1 : 3 * h + 2]], axis=0)
    top = share[:h, : 2 * h]
    bottom = jnp.concatenate([top[:, h:].T, share[:h, 2 * h : 3 * h]], axis=1)
    solve = math.sqrt(total) * inverse_factor(jnp.concatenate([top, bottom], axis=0))
    out_ref[...] = times(solve, thirds(images - mean))


def call(kernel, args, out_shape, in_specs=None):
    return pl.pallas_call(
        kernel,
        out_shape=out_shape,
        in_specs=in_specs or [VMEM] * len(args),
        out_specs=jax.tree.map(lambda _: VMEM, out_shape),
        compiler_params=pltpu.CompilerParams(vmem_limit_bytes=24 * 2**20),
    )(*args)


def after(value, *others):
    return lax.optimization_barrier((value, *others))[0]


def exchange(axis, offset, size=4):
    return lambda value: lax.ppermute(value, axis, [(i, i ^ offset) for i in range(size)])


CORE, CHIP = exchange("row", 1), exchange("row", 2)
NEAR, FAR, OPPOSITE = exchange("col", 1), exchange("col", 2), exchange("col", 3)


def middle(value):
    return lax.ppermute(value, "col", MIDDLE)


def diagonal(value):
    return lax.ppermute(value, ("row", "col"), [(4 * r + c, 4 * (r ^ 2) + 3 - c) for r in range(4) for c in (1, 2)])


MIDDLE = [(1, 2), (2, 1)]


def local(corpus, sample_rows, initial):
    vecs, size = initial.shape
    half = size // 2
    count = 16
    total = float(size * count)
    scale = UNIT * UNIT / (2.0 * corpus.shape[1])
    levels = call(encode, [initial], jax.ShapeDtypeStruct((vecs // 2 + 8, size), jnp.int32))
    landmarks = lax.gather(
        corpus,
        sample_rows[:, None],
        lax.GatherDimensionNumbers(offset_dims=(1,), collapsed_slice_dims=(0,), start_index_map=(0,)),
        (1, corpus.shape[1]),
        mode="promise_in_bounds",
    )
    code = jnp.round(landmarks * (1.0 / UNIT)).astype(jnp.int32)
    own = jnp.concatenate([pair(code[:half], code[half:]), levels], axis=0)

    def build(*blocks):
        shapes = jax.ShapeDtypeStruct((len(blocks) * size, 2 * size), BF16), jax.ShapeDtypeStruct((vecs, len(blocks) * size), F32)
        tile, start = call(functools.partial(build_kernel, half, scale), [*side, *blocks], shapes)
        tiles.append(tile)
        starts.append(start)

    outer, partner, chip = NEAR(own), middle(own), CHIP(own)
    tiles, starts = [], []
    groups = [[own, outer, CORE(own), CORE(outer)]]
    codes = jax.ShapeDtypeStruct((2 * size, corpus.shape[1]), BF16)
    side = call(functools.partial(side_kernel, half, scale), [own, outer], (codes, codes, jax.ShapeDtypeStruct((1, 2 * size), F32)))
    build(*groups[0])
    partner_outer, chip_outer, chip_partner = middle(outer), NEAR(chip), CHIP(partner)
    groups.append([partner, CORE(partner), chip, CORE(chip)])
    build(*groups[1])
    chip_partner_outer = CHIP(after(partner_outer, tiles[0]))
    groups.append([partner_outer, CORE(partner_outer), chip_outer, CORE(chip_outer)])
    build(*groups[2])
    groups.append([chip_partner, CORE(chip_partner)])
    build(*groups[3])
    final = CORE(after(chip_partner_outer, *tiles[1:4]))
    groups.append([chip_partner_outer])
    build(*groups[4])
    images, tile = call(
        functools.partial(first_kernel, len(tiles), half, scale, total),
        [*side, final, *tiles, *starts],
        (jax.ShapeDtypeStruct((vecs, 2 * size), F32), jax.ShapeDtypeStruct((size, 2 * size), BF16)),
    )
    tiles.append(tile)
    there, beside = middle(images), CHIP(images)
    beyond = diagonal(images)
    gathered = [images, there, beside, beyond]
    gathered += [CORE(value) for value in gathered]
    here, part, chip, far = 0, 1, 2, 3
    pieces = [(here, 0), (here, 1), (here + 4, 0), (here + 4, 1), (part, 0), (part + 4, 0), (chip, 0), (chip + 4, 0)]
    pieces += [(part, 1), (part + 4, 1), (chip, 1), (chip + 4, 1), (far, 0), (far + 4, 0), (far, 1), (far + 4, 1)]
    block = jax.ShapeDtypeStruct((vecs, size), F32)
    packed = jax.ShapeDtypeStruct((vecs // 2 + 8, 2 * vecs), F32)
    images, other, share = call(functools.partial(second_kernel, pieces, total), gathered + tiles, (block, block, packed))
    given = NEAR(other)
    for step, swap in enumerate((CORE, CHIP)):
        share = call(functools.partial(merge_kernel, 2.0 * size * 2**step), [share, swap(share)], packed)
    place = lax.axis_index("col")
    flag = ((place == 0) | (place == 3)).astype(jnp.int32).reshape(1)
    return call(
        functools.partial(last_kernel, total),
        [flag, share, NEAR(share), FAR(share), OPPOSITE(share), images, given],
        block,
        [pl.BlockSpec(memory_space=pltpu.SMEM)] + [VMEM] * 6,
    )


def local_large(corpus, sample_rows, initial):
    both = ("row", "col")
    landmarks = corpus[sample_rows]
    everyone = lax.all_gather(landmarks, both, axis=0, tiled=True)
    total = float(everyone.shape[0])
    norms = jnp.sum(everyone * everyone, axis=1)
    own_norms = jnp.sum(landmarks * landmarks, axis=1)
    products = jnp.dot(everyone, landmarks.T, precision=HIGHEST, preferred_element_type=F32)
    tile = jnp.exp(-(norms[:, None] + own_norms[None, :] - 2.0 * products) / (2.0 * corpus.shape[1])).astype(BF16)
    starts = lax.all_gather(initial, both, axis=1, tiled=True)
    rounded = (starts - jnp.mean(starts, axis=1, keepdims=True)).astype(BF16)
    vectors = None
    for _ in range(ITERS):
        images = jnp.dot(rounded, tile, preferred_element_type=F32)
        gathered = lax.all_gather(images, both, axis=1, tiled=True)
        mean = jnp.mean(gathered, axis=1, keepdims=True)
        centered = gathered - mean
        factor = jnp.linalg.cholesky(jnp.dot(centered, centered.T, precision=HIGHEST))
        rounded = (math.sqrt(total) * jax.scipy.linalg.solve_triangular(factor, centered, lower=True)).astype(BF16)
        vectors = math.sqrt(total) * jax.scipy.linalg.solve_triangular(factor, images - mean, lower=True)
    return vectors


def solution(mesh):
    shape = mesh.shape
    whole = P(("groups", "row", "col"))
    return jax.shard_map(
        local if (shape["row"], shape["col"]) == (4, 4) else local_large,
        mesh=mesh,
        in_specs=(P(("groups", "row", "col"), None), whole, P(None, ("groups", "row", "col"))),
        out_specs=P(None, ("groups", "row", "col")),
        check_vma=False,
    )
```

```python
import functools
import math

import jax
import jax.numpy as jnp
from jax import lax
from jax.experimental import pallas as pl
from jax.experimental.pallas import tpu as pltpu
from jax.sharding import PartitionSpec as P

ITERS = 2
REACH = 20.0
UNIT = REACH / 32767.0
FIXED, RANGE = 2.0**28, 2.0**26
HIGHEST = lax.Precision.HIGHEST
BF16, F32 = jnp.bfloat16, jnp.float32
VMEM = pl.BlockSpec(memory_space=pltpu.VMEM)


def matmul(a, b, contract, precision=None):
    return lax.dot_general(a, b, ((contract[:1], contract[1:]), ((), ())), precision=precision, preferred_element_type=F32)


def pair(high, low):
    return (high << 16) | (low & 0xFFFF)


def unpair(words):
    return words >> 16, (words << 16) >> 16


def encode(initial_ref, out_ref):
    initial = initial_ref[...]
    vecs, size = initial.shape
    half = size // 2
    mean = jnp.round(jnp.sum(initial, axis=1, keepdims=True) * (FIXED / size)).astype(jnp.int32)
    apart = initial - mean.astype(F32) * (1.0 / FIXED)
    reach = jnp.ceil(jnp.max(jnp.abs(apart), axis=1, keepdims=True) * RANGE).astype(jnp.int32) + 1
    step = reach.astype(F32) * (1.0 / (RANGE * 32767.0))
    level = jnp.round(apart / step).astype(jnp.int32)
    words = pair(level[:, :half], level[:, half:])
    row = lax.broadcasted_iota(jnp.int32, (vecs, size), 0)
    lane = lax.broadcasted_iota(jnp.int32, (vecs, size), 1)
    header = jnp.where(lane == row, mean, jnp.where(lane == row + vecs, reach, 0))
    out_ref[: vecs // 2] = jnp.concatenate([words[: vecs // 2], words[vecs // 2 :]], axis=1)
    out_ref[vecs // 2 :] = jnp.broadcast_to(jnp.sum(header, axis=0, keepdims=True), (8, size))


def decode(block, half):
    words = block[half : block.shape[0] - 8]
    vecs = 2 * words.shape[0]
    level = jnp.concatenate([jnp.concatenate(unpair(part), axis=1) for part in (words[:, :half], words[:, half:])], axis=0)
    header = block[block.shape[0] - 8 :].astype(F32)[:1, : 2 * vecs]
    row = lax.broadcasted_iota(jnp.int32, (vecs, 2 * vecs), 0)
    lane = lax.broadcasted_iota(jnp.int32, (vecs, 2 * vecs), 1)
    mean = jnp.sum(jnp.where(lane == row, header, 0.0), axis=1, keepdims=True) * (1.0 / FIXED)
    step = jnp.sum(jnp.where(lane == row + vecs, header, 0.0), axis=1, keepdims=True) * (1.0 / (RANGE * 32767.0))
    return level.astype(F32) * step + mean


def split_codes(words):
    code = jnp.concatenate(unpair(words), axis=0)
    high = ((code + 128) >> 8) << 8
    return high.astype(F32).astype(BF16), (code - high).astype(F32).astype(BF16)


def kernel_rows(words, own_high, own_low, own_norms, scale):
    high, low = split_codes(words)
    wide = high.astype(F32) + low.astype(F32)
    norms = scale * jnp.sum(wide * wide, axis=1, keepdims=True)
    dots = matmul(high, own_high, (1, 1)) + (matmul(high, own_low, (1, 1)) + matmul(low, own_high, (1, 1))) + matmul(low, own_low, (1, 1))
    return jnp.exp((2.0 * scale) * dots - (norms + own_norms)).astype(BF16)


def own_side(refs, half, scale):
    parts = [split_codes(ref[:half]) for ref in refs]
    high = jnp.concatenate([part[0] for part in parts], axis=0)
    low = jnp.concatenate([part[1] for part in parts], axis=0)
    wide = high.astype(F32) + low.astype(F32)
    norms = matmul(jnp.ones((8, wide.shape[1]), F32), wide * wide, (1, 1), HIGHEST)[:1]
    return high, low, scale * norms


def side_kernel(half, scale, own_ref, outer_ref, high_ref, low_ref, norms_ref):
    high_ref[...], low_ref[...], norms_ref[...] = own_side((own_ref, outer_ref), half, scale)


def build_kernel(half, scale, *refs):
    side, blocks, (tile_ref, start_ref) = refs[:3], refs[3:-2], refs[-2:]
    for b, block in enumerate(blocks):
        place = pl.ds(b * 2 * half, 2 * half)
        tile_ref[place, :] = kernel_rows(block[:half], *(ref[...] for ref in side), scale)
        start_ref[:, place] = decode(block[...], half)


def first_kernel(count, half, scale, total, *refs):
    side, block, tiles, parts = refs[:3], refs[3], refs[4 : 4 + count], refs[4 + count : -2]
    out_ref, tile_ref = refs[-2:]
    size = 2 * half
    tile_ref[...] = kernel_rows(block[:half], *(ref[...] for ref in side), scale)
    starts = [part[...] for part in parts] + [decode(block[...], half)]
    pieces = [start[:, b : b + size] for start in starts for b in range(0, start.shape[1], size)]
    sums = pieces[0]
    for piece in pieces[1:]:
        sums = sums + piece
    mean = jnp.sum(sums, axis=1, keepdims=True) / total
    images = None
    for start, tile in zip(starts, (*tiles, tile_ref)):
        term = matmul((start - mean).astype(BF16), tile[...], (1, 0))
        images = term if images is None else images + term
    out_ref[...] = images


def inverse_factor(gram):
    n = gram.shape[0]
    row_id = lax.broadcasted_iota(jnp.int32, (n, 2 * n), 0)
    col_id = lax.broadcasted_iota(jnp.int32, (n, 2 * n), 1)
    eye = (row_id[:, :n] == col_id[:, :n]).astype(F32)
    work = jnp.concatenate([gram, eye], axis=1)
    done = []
    for top in range(0, n, 8):
        rows = n - top
        place = lax.broadcasted_iota(jnp.int32, (rows, 2 * n), 0)
        columns = [jnp.broadcast_to(work[:, top + k : top + k + 1], (rows, 2 * n)) for k in range(8)]
        for k in range(0, 8, 2):
            one, two = columns[k], columns[k + 1]
            a, b, d = one[k : k + 1], one[k + 1 : k + 2], two[k + 1 : k + 2]
            inverse = 1.0 / a
            slope = b * inverse
            second = jnp.where(place > k + 1, (two * a - one * b) * (1.0 / (a * d - b * b)), 0.0)
            first = jnp.where(place > k, one, 0.0)

            def eliminate(value):
                upper = value[k : k + 1]
                return value - first * (upper * inverse) - second * (value[k + 1 : k + 2] - slope * upper)

            work = eliminate(work)
            columns = columns[: k + 2] + [eliminate(column) for column in columns[k + 2 :]]
        done.append(work[:8])
        work = work[8:]
    upper = jnp.concatenate(done, axis=0)
    pivots = jnp.sum(jnp.where(row_id == col_id, upper, 0.0), axis=1, keepdims=True)
    return upper[:, n:] * lax.rsqrt(pivots)


def thirds(value):
    high = value.astype(BF16)
    rest = value - high.astype(F32)
    middle = rest.astype(BF16)
    return jnp.concatenate([high, middle, (rest - middle.astype(F32)).astype(BF16)], axis=0)


def gram_of(stack):
    n = stack.shape[0] // 3
    p = matmul(stack, stack, (1, 1))
    middle = p[n : 2 * n, n : 2 * n] + (p[:n, 2 * n :] + p[2 * n :, :n])
    return p[:n, :n] + ((p[:n, n : 2 * n] + p[n : 2 * n, :n]) + middle)


def times(matrix, stack):
    n = matrix.shape[0]
    parts = thirds(matrix)
    p = matmul(jnp.concatenate([parts, parts, parts], axis=1), stack, (1, 0))
    return p[:n] + (p[n : 2 * n] + p[2 * n :])


def partial_kernel(count, *refs):
    shift_ref, images = refs[0], refs[1 : 1 + count]
    stack_ref, gram_ref, sum_ref = refs[-3:]
    value = jnp.concatenate([image[...] for image in images], axis=1) - shift_of(shift_ref)
    stack = thirds(value)
    stack_ref[...] = stack
    gram_ref[...] = gram_of(stack)
    sum_ref[...] = jnp.broadcast_to(jnp.sum(value, axis=1, keepdims=True), sum_ref.shape)


def shift_of(ref):
    return jnp.sum(ref[...], axis=1, keepdims=True) * (1.0 / ref.shape[1])


def second_kernel(parts, pieces, total, *refs):
    shift_ref, images = refs[0], refs[1:3]
    stacks, grams, sums = (refs[3 + i * parts : 3 + (i + 1) * parts] for i in range(3))
    tiles = refs[3 + 3 * parts : -3]
    own_ref, other_ref, share_ref = refs[-3:]
    size = own_ref.shape[1]
    value = jnp.concatenate([image[...] for image in images], axis=1) - shift_of(shift_ref)
    stack = thirds(value)
    gram = gram_of(stack)
    far = jnp.sum(value, axis=1, keepdims=True)
    for part, sum_part in zip(grams, sums):
        gram, far = gram + part[...], far + sum_part[:, :1]
    far = far * (1.0 / total)
    n = gram.shape[0]
    eye = lax.broadcasted_iota(jnp.int32, (n, n), 0) == lax.broadcasted_iota(jnp.int32, (n, n), 1)
    gram = gram - (total * far) * jnp.sum(jnp.where(eye, far, 0.0), axis=0, keepdims=True)
    solve = math.sqrt(total) * inverse_factor(gram)
    level = times(solve, thirds(jnp.broadcast_to(far, (n, 2 * n))))[:, :1]
    vectors = []
    for part in (*stacks, None):
        whole = stack if part is None else part[...]
        vectors.append((times(solve, whole) - level).astype(BF16))
    vectors = jnp.concatenate(vectors, axis=1)
    vectors = jnp.concatenate([vectors[:, p * size : (p + 1) * size] for p in pieces], axis=1)
    result, begin = None, 0
    for tile in tiles:
        end = begin + tile.shape[0]
        term = matmul(vectors[:, begin:end], tile[...], (1, 0))
        result, begin = term if result is None else result + term, end
    own_ref[...] = result[:, :size]
    other_ref[...] = result[:, size:]
    local_mean = jnp.sum(result, axis=1, keepdims=True) / (2 * size)
    gram = gram_of(thirds(result - local_mean))
    h = n // 2
    across = jnp.sum(jnp.where(eye, local_mean, 0.0), axis=0, keepdims=True)
    share_ref[:h] = jnp.concatenate([gram[:h], gram[h:, h:], local_mean[:h], local_mean[h:], jnp.zeros((h, h - 2), F32)], axis=1)
    share_ref[h:] = jnp.broadcast_to(jnp.concatenate([across, across[:, h:], jnp.zeros((1, h), F32)], axis=1), (8, 4 * h))


def merge(a, b, each):
    h = a.shape[0] - 8
    apart = a - b
    lane = lax.broadcasted_iota(jnp.int32, (h, 4 * h), 1)
    down = jnp.where(lane < 2 * h, apart[:h, 3 * h : 3 * h + 1], apart[:h, 3 * h + 1 : 3 * h + 2])
    both = a + b
    top = jnp.where(lane < 3 * h, both[:h] + (0.5 * each) * (down * apart[h : h + 1]), 0.5 * both[:h])
    return jnp.concatenate([top, 0.5 * both[h:]], axis=0)


def merge_kernel(each, a_ref, b_ref, out_ref):
    out_ref[...] = merge(a_ref[...], b_ref[...], each)


def last_kernel(total, outer_ref, share_ref, near_ref, far_ref, across_ref, own_ref, given_ref, out_ref):
    outer = outer_ref[0] == 1
    first = jnp.where(outer, near_ref[...], share_ref[...])
    second = jnp.where(outer, far_ref[...], across_ref[...])
    images = jnp.where(outer, given_ref[...], own_ref[...])
    share = merge(first, second, 0.5 * total)
    h = share.shape[0] - 8
    mean = jnp.concatenate([share[:h, 3 * h : 3 * h + 1], share[:h, 3 * h + 1 : 3 * h + 2]], axis=0)
    top = share[:h, : 2 * h]
    bottom = jnp.concatenate([top[:, h:].T, share[:h, 2 * h : 3 * h]], axis=1)
    solve = math.sqrt(total) * inverse_factor(jnp.concatenate([top, bottom], axis=0))
    out_ref[...] = times(solve, thirds(images - mean))


def call(kernel, args, out_shape, in_specs=None):
    return pl.pallas_call(
        kernel,
        out_shape=out_shape,
        in_specs=in_specs or [VMEM] * len(args),
        out_specs=jax.tree.map(lambda _: VMEM, out_shape),
        compiler_params=pltpu.CompilerParams(vmem_limit_bytes=24 * 2**20),
    )(*args)


def after(value, *others):
    return lax.optimization_barrier((value, *others))[0]


def exchange(axis, offset, size=4):
    return lambda value: lax.ppermute(value, axis, [(i, i ^ offset) for i in range(size)])


CORE, CHIP = exchange("row", 1), exchange("row", 2)
NEAR, FAR, OPPOSITE = exchange("col", 1), exchange("col", 2), exchange("col", 3)


def middle(value):
    return lax.ppermute(value, "col", MIDDLE)


def diagonal(value):
    return lax.ppermute(value, ("row", "col"), [(4 * r + c, 4 * (r ^ 2) + 3 - c) for r in range(4) for c in (1, 2)])


MIDDLE = [(1, 2), (2, 1)]


def local(corpus, sample_rows, initial):
    vecs, size = initial.shape
    half = size // 2
    count = 16
    total = float(size * count)
    scale = UNIT * UNIT / (2.0 * corpus.shape[1])
    levels = call(encode, [initial], jax.ShapeDtypeStruct((vecs // 2 + 8, size), jnp.int32))
    landmarks = lax.gather(
        corpus,
        sample_rows[:, None],
        lax.GatherDimensionNumbers(offset_dims=(1,), collapsed_slice_dims=(0,), start_index_map=(0,)),
        (1, corpus.shape[1]),
        mode="promise_in_bounds",
    )
    code = jnp.round(landmarks * (1.0 / UNIT)).astype(jnp.int32)
    own = jnp.concatenate([pair(code[:half], code[half:]), levels], axis=0)

    def build(*blocks):
        shapes = jax.ShapeDtypeStruct((len(blocks) * size, 2 * size), BF16), jax.ShapeDtypeStruct((vecs, len(blocks) * size), F32)
        tile, start = call(functools.partial(build_kernel, half, scale), [*side, *blocks], shapes)
        tiles.append(tile)
        starts.append(start)

    outer, partner, chip = NEAR(own), middle(own), CHIP(own)
    tiles, starts = [], []
    groups = [[own, outer, CORE(own), CORE(outer)]]
    codes = jax.ShapeDtypeStruct((2 * size, corpus.shape[1]), BF16)
    side = call(functools.partial(side_kernel, half, scale), [own, outer], (codes, codes, jax.ShapeDtypeStruct((1, 2 * size), F32)))
    build(*groups[0])
    partner_outer, chip_outer, chip_partner = middle(outer), NEAR(chip), CHIP(partner)
    groups.append([partner, CORE(partner), chip, CORE(chip)])
    build(*groups[1])
    chip_partner_outer = CHIP(after(partner_outer, tiles[0]))
    build(partner_outer, CORE(partner_outer))
    build(chip_partner, CORE(chip_partner))
    final = CORE(after(chip_partner_outer, *tiles[1:3]))
    build(chip_outer, CORE(chip_outer))
    build(chip_partner_outer)
    images, tile = call(
        functools.partial(first_kernel, len(tiles), half, scale, total),
        [*side, final, *tiles, *starts],
        (jax.ShapeDtypeStruct((vecs, 2 * size), F32), jax.ShapeDtypeStruct((size, 2 * size), BF16)),
    )
    tiles.append(tile)
    places = [images, middle(images), CHIP(images), diagonal(images)]
    pairs = [[value, CORE(value)] for value in places]
    block = jax.ShapeDtypeStruct((vecs, size), F32)
    parts = []
    for group in ([0, 1, 2],):
        values = [value for p in group for value in pairs[p]]
        shapes = jax.ShapeDtypeStruct((3 * vecs, len(values) * 2 * size), BF16), jax.ShapeDtypeStruct((vecs, vecs), F32)
        parts.append(call(functools.partial(partial_kernel, len(values)), [images, *values], (*shapes, jax.ShapeDtypeStruct((vecs, 128), F32))))
    here, part, chip, far = (4 * p for p in range(4))
    pieces = [here, here + 1, here + 2, here + 3, part, part + 2, chip, chip + 2]
    pieces += [part + 1, part + 3, far, far + 2, chip + 1, chip + 3, far + 1, far + 3]
    packed = jax.ShapeDtypeStruct((vecs // 2 + 8, 2 * vecs), F32)
    known = [part[i] for i in range(3) for part in parts]
    images, other, share = call(
        functools.partial(second_kernel, len(parts), pieces, total), [images, *pairs[3], *known, *tiles], (block, block, packed)
    )
    given = NEAR(other)
    for step, swap in enumerate((CORE, CHIP)):
        share = call(functools.partial(merge_kernel, 2.0 * size * 2**step), [share, swap(share)], packed)
    place = lax.axis_index("col")
    flag = ((place == 0) | (place == 3)).astype(jnp.int32).reshape(1)
    return call(
        functools.partial(last_kernel, total),
        [flag, share, NEAR(share), FAR(share), OPPOSITE(share), images, given],
        block,
        [pl.BlockSpec(memory_space=pltpu.SMEM)] + [VMEM] * 6,
    )


def local_large(corpus, sample_rows, initial):
    both = ("row", "col")
    landmarks = corpus[sample_rows]
    everyone = lax.all_gather(landmarks, both, axis=0, tiled=True)
    total = float(everyone.shape[0])
    norms = jnp.sum(everyone * everyone, axis=1)
    own_norms = jnp.sum(landmarks * landmarks, axis=1)
    products = jnp.dot(everyone, landmarks.T, precision=HIGHEST, preferred_element_type=F32)
    tile = jnp.exp(-(norms[:, None] + own_norms[None, :] - 2.0 * products) / (2.0 * corpus.shape[1])).astype(BF16)
    starts = lax.all_gather(initial, both, axis=1, tiled=True)
    rounded = (starts - jnp.mean(starts, axis=1, keepdims=True)).astype(BF16)
    vectors = None
    for _ in range(ITERS):
        images = jnp.dot(rounded, tile, preferred_element_type=F32)
        gathered = lax.all_gather(images, both, axis=1, tiled=True)
        mean = jnp.mean(gathered, axis=1, keepdims=True)
        centered = gathered - mean
        factor = jnp.linalg.cholesky(jnp.dot(centered, centered.T, precision=HIGHEST))
        rounded = (math.sqrt(total) * jax.scipy.linalg.solve_triangular(factor, centered, lower=True)).astype(BF16)
        vectors = math.sqrt(total) * jax.scipy.linalg.solve_triangular(factor, images - mean, lower=True)
    return vectors


def solution(mesh):
    shape = mesh.shape
    whole = P(("groups", "row", "col"))
    return jax.shard_map(
        local if (shape["row"], shape["col"]) == (4, 4) else local_large,
        mesh=mesh,
        in_specs=(P(("groups", "row", "col"), None), whole, P(None, ("groups", "row", "col"))),
        out_specs=P(None, ("groups", "row", "col")),
        check_vma=False,
    )
```

```python
import functools
import math

import jax
import jax.numpy as jnp
from jax import lax
from jax.experimental import pallas as pl
from jax.experimental.pallas import tpu as pltpu
from jax.sharding import PartitionSpec as P

ITERS = 2
REACH = 20.0
UNIT = REACH / 32767.0
FIXED, RANGE = 2.0**28, 2.0**26
HIGHEST = lax.Precision.HIGHEST
BF16, F32 = jnp.bfloat16, jnp.float32
VMEM = pl.BlockSpec(memory_space=pltpu.VMEM)


def matmul(a, b, contract, precision=None):
    return lax.dot_general(a, b, ((contract[:1], contract[1:]), ((), ())), precision=precision, preferred_element_type=F32)


def pair(high, low):
    return (high << 16) | (low & 0xFFFF)


def unpair(words):
    return words >> 16, (words << 16) >> 16


def encode(initial_ref, out_ref):
    initial = initial_ref[...]
    vecs, size = initial.shape
    half = size // 2
    mean = jnp.round(jnp.sum(initial, axis=1, keepdims=True) * (FIXED / size)).astype(jnp.int32)
    apart = initial - mean.astype(F32) * (1.0 / FIXED)
    reach = jnp.ceil(jnp.max(jnp.abs(apart), axis=1, keepdims=True) * RANGE).astype(jnp.int32) + 1
    step = reach.astype(F32) * (1.0 / (RANGE * 32767.0))
    level = jnp.round(apart / step).astype(jnp.int32)
    words = pair(level[:, :half], level[:, half:])
    row = lax.broadcasted_iota(jnp.int32, (vecs, size), 0)
    lane = lax.broadcasted_iota(jnp.int32, (vecs, size), 1)
    header = jnp.where(lane == row, mean, jnp.where(lane == row + vecs, reach, 0))
    out_ref[: vecs // 2] = jnp.concatenate([words[: vecs // 2], words[vecs // 2 :]], axis=1)
    out_ref[vecs // 2 :] = jnp.broadcast_to(jnp.sum(header, axis=0, keepdims=True), (8, size))


def decode(block, half):
    words = block[half : block.shape[0] - 8]
    vecs = 2 * words.shape[0]
    level = jnp.concatenate([jnp.concatenate(unpair(part), axis=1) for part in (words[:, :half], words[:, half:])], axis=0)
    header = block[block.shape[0] - 8 :].astype(F32)[:1, : 2 * vecs]
    row = lax.broadcasted_iota(jnp.int32, (vecs, 2 * vecs), 0)
    lane = lax.broadcasted_iota(jnp.int32, (vecs, 2 * vecs), 1)
    mean = jnp.sum(jnp.where(lane == row, header, 0.0), axis=1, keepdims=True) * (1.0 / FIXED)
    step = jnp.sum(jnp.where(lane == row + vecs, header, 0.0), axis=1, keepdims=True) * (1.0 / (RANGE * 32767.0))
    return level.astype(F32) * step + mean


def split_codes(words):
    code = jnp.concatenate(unpair(words), axis=0)
    high = ((code + 128) >> 8) << 8
    return high.astype(F32).astype(BF16), (code - high).astype(F32).astype(BF16)


def kernel_rows(words, own_high, own_low, own_norms, scale):
    high, low = split_codes(words)
    wide = high.astype(F32) + low.astype(F32)
    norms = scale * jnp.sum(wide * wide, axis=1, keepdims=True)
    dots = matmul(high, own_high, (1, 1)) + (matmul(high, own_low, (1, 1)) + matmul(low, own_high, (1, 1))) + matmul(low, own_low, (1, 1))
    return jnp.exp((2.0 * scale) * dots - (norms + own_norms)).astype(BF16)


def own_side(refs, half, scale):
    parts = [split_codes(ref[:half]) for ref in refs]
    high = jnp.concatenate([part[0] for part in parts], axis=0)
    low = jnp.concatenate([part[1] for part in parts], axis=0)
    wide = high.astype(F32) + low.astype(F32)
    norms = matmul(jnp.ones((8, wide.shape[1]), F32), wide * wide, (1, 1), HIGHEST)[:1]
    return high, low, scale * norms


def side_kernel(half, scale, own_ref, outer_ref, high_ref, low_ref, norms_ref):
    high_ref[...], low_ref[...], norms_ref[...] = own_side((own_ref, outer_ref), half, scale)


def build_kernel(half, scale, *refs):
    side, blocks, (tile_ref, start_ref) = refs[:3], refs[3:-2], refs[-2:]
    for b, block in enumerate(blocks):
        place = pl.ds(b * 2 * half, 2 * half)
        tile_ref[place, :] = kernel_rows(block[:half], *(ref[...] for ref in side), scale)
        start_ref[:, place] = decode(block[...], half)


def first_kernel(count, half, scale, total, *refs):
    side, block, tiles, parts = refs[:3], refs[3], refs[4 : 4 + count], refs[4 + count : -2]
    out_ref, tile_ref = refs[-2:]
    size = 2 * half
    tile_ref[...] = kernel_rows(block[:half], *(ref[...] for ref in side), scale)
    starts = [part[...] for part in parts] + [decode(block[...], half)]
    pieces = [start[:, b : b + size] for start in starts for b in range(0, start.shape[1], size)]
    sums = pieces[0]
    for piece in pieces[1:]:
        sums = sums + piece
    mean = jnp.sum(sums, axis=1, keepdims=True) / total
    images = None
    for start, tile in zip(starts, (*tiles, tile_ref)):
        term = matmul((start - mean).astype(BF16), tile[...], (1, 0))
        images = term if images is None else images + term
    out_ref[...] = images


def inverse_factor(gram):
    n = gram.shape[0]
    row_id = lax.broadcasted_iota(jnp.int32, (n, 2 * n), 0)
    col_id = lax.broadcasted_iota(jnp.int32, (n, 2 * n), 1)
    eye = (row_id[:, :n] == col_id[:, :n]).astype(F32)
    work = jnp.concatenate([gram, eye], axis=1)
    done = []
    for top in range(0, n, 8):
        rows = n - top
        place = lax.broadcasted_iota(jnp.int32, (rows, 2 * n), 0)
        columns = [jnp.broadcast_to(work[:, top + k : top + k + 1], (rows, 2 * n)) for k in range(8)]
        for k in range(0, 8, 2):
            one, two = columns[k], columns[k + 1]
            a, b, d = one[k : k + 1], one[k + 1 : k + 2], two[k + 1 : k + 2]
            inverse = 1.0 / a
            slope = b * inverse
            second = jnp.where(place > k + 1, (two * a - one * b) * (1.0 / (a * d - b * b)), 0.0)
            first = jnp.where(place > k, one, 0.0)

            def eliminate(value):
                upper = value[k : k + 1]
                return value - first * (upper * inverse) - second * (value[k + 1 : k + 2] - slope * upper)

            work = eliminate(work)
            columns = columns[: k + 2] + [eliminate(column) for column in columns[k + 2 :]]
        done.append(work[:8])
        work = work[8:]
    upper = jnp.concatenate(done, axis=0)
    pivots = jnp.sum(jnp.where(row_id == col_id, upper, 0.0), axis=1, keepdims=True)
    return upper[:, n:] * lax.rsqrt(pivots)


def thirds(value):
    high = value.astype(BF16)
    rest = value - high.astype(F32)
    middle = rest.astype(BF16)
    return jnp.concatenate([high, middle, (rest - middle.astype(F32)).astype(BF16)], axis=0)


def gram_of(stack):
    n = stack.shape[0] // 3
    p = matmul(stack, stack, (1, 1))
    middle = p[n : 2 * n, n : 2 * n] + (p[:n, 2 * n :] + p[2 * n :, :n])
    return p[:n, :n] + ((p[:n, n : 2 * n] + p[n : 2 * n, :n]) + middle)


def times(matrix, stack):
    n = matrix.shape[0]
    parts = thirds(matrix)
    p = matmul(jnp.concatenate([parts, parts, parts], axis=1), stack, (1, 0))
    return p[:n] + (p[n : 2 * n] + p[2 * n :])


def partial_kernel(count, *refs):
    shift_ref, images = refs[0], refs[1 : 1 + count]
    stack_ref, gram_ref, sum_ref = refs[-3:]
    value = jnp.concatenate([image[...] for image in images], axis=1) - shift_of(shift_ref)
    stack = thirds(value)
    stack_ref[...] = stack
    gram_ref[...] = gram_of(stack)
    sum_ref[...] = jnp.broadcast_to(jnp.sum(value, axis=1, keepdims=True), sum_ref.shape)


def shift_of(ref):
    return jnp.sum(ref[...], axis=1, keepdims=True) * (1.0 / ref.shape[1])


def second_kernel(parts, pieces, total, *refs):
    shift_ref, images = refs[0], refs[1:3]
    stacks, grams, sums = (refs[3 + i * parts : 3 + (i + 1) * parts] for i in range(3))
    tiles = refs[3 + 3 * parts : -3]
    own_ref, other_ref, share_ref = refs[-3:]
    size = own_ref.shape[1]
    value = jnp.concatenate([image[...] for image in images], axis=1) - shift_of(shift_ref)
    stack = thirds(value)
    gram = gram_of(stack)
    far = jnp.sum(value, axis=1, keepdims=True)
    for part, sum_part in zip(grams, sums):
        gram, far = gram + part[...], far + sum_part[:, :1]
    far = far * (1.0 / total)
    n = gram.shape[0]
    eye = lax.broadcasted_iota(jnp.int32, (n, n), 0) == lax.broadcasted_iota(jnp.int32, (n, n), 1)
    gram = gram - (total * far) * jnp.sum(jnp.where(eye, far, 0.0), axis=0, keepdims=True)
    solve = math.sqrt(total) * inverse_factor(gram)
    level = times(solve, thirds(jnp.broadcast_to(far, (n, 2 * n))))[:, :1]
    vectors = []
    for part in (*stacks, None):
        whole = stack if part is None else part[...]
        vectors.append((times(solve, whole) - level).astype(BF16))
    vectors = jnp.concatenate(vectors, axis=1)
    vectors = jnp.concatenate([vectors[:, p * size : (p + 1) * size] for p in pieces], axis=1)
    result, begin = None, 0
    for tile in tiles:
        end = begin + tile.shape[0]
        term = matmul(vectors[:, begin:end], tile[...], (1, 0))
        result, begin = term if result is None else result + term, end
    own_ref[...] = result[:, :size]
    other_ref[...] = result[:, size:]
    local_mean = jnp.sum(result, axis=1, keepdims=True) / (2 * size)
    gram = gram_of(thirds(result - local_mean))
    h = n // 2
    across = jnp.sum(jnp.where(eye, local_mean, 0.0), axis=0, keepdims=True)
    share_ref[:h] = jnp.concatenate([gram[:h], gram[h:, h:], local_mean[:h], local_mean[h:], jnp.zeros((h, h - 2), F32)], axis=1)
    share_ref[h:] = jnp.broadcast_to(jnp.concatenate([across, across[:, h:], jnp.zeros((1, h), F32)], axis=1), (8, 4 * h))


def merge(a, b, each):
    h = a.shape[0] - 8
    apart = a - b
    lane = lax.broadcasted_iota(jnp.int32, (h, 4 * h), 1)
    down = jnp.where(lane < 2 * h, apart[:h, 3 * h : 3 * h + 1], apart[:h, 3 * h + 1 : 3 * h + 2])
    both = a + b
    top = jnp.where(lane < 3 * h, both[:h] + (0.5 * each) * (down * apart[h : h + 1]), 0.5 * both[:h])
    return jnp.concatenate([top, 0.5 * both[h:]], axis=0)


def merge_kernel(each, a_ref, b_ref, out_ref):
    out_ref[...] = merge(a_ref[...], b_ref[...], each)


def column_kernel(each, outer_ref, share_ref, near_ref, far_ref, across_ref, out_ref):
    outer = outer_ref[0] == 1
    first = jnp.where(outer, near_ref[...], share_ref[...])
    out_ref[...] = merge(first, jnp.where(outer, far_ref[...], across_ref[...]), each)


def last_kernel(total, outer_ref, share_ref, beside_ref, own_ref, given_ref, out_ref):
    images = jnp.where(outer_ref[0] == 1, given_ref[...], own_ref[...])
    share = merge(share_ref[...], beside_ref[...], 0.5 * total)
    h = share.shape[0] - 8
    mean = jnp.concatenate([share[:h, 3 * h : 3 * h + 1], share[:h, 3 * h + 1 : 3 * h + 2]], axis=0)
    top = share[:h, : 2 * h]
    bottom = jnp.concatenate([top[:, h:].T, share[:h, 2 * h : 3 * h]], axis=1)
    solve = math.sqrt(total) * inverse_factor(jnp.concatenate([top, bottom], axis=0))
    out_ref[...] = times(solve, thirds(images - mean))


def call(kernel, args, out_shape, in_specs=None):
    return pl.pallas_call(
        kernel,
        out_shape=out_shape,
        in_specs=in_specs or [VMEM] * len(args),
        out_specs=jax.tree.map(lambda _: VMEM, out_shape),
        compiler_params=pltpu.CompilerParams(vmem_limit_bytes=24 * 2**20),
    )(*args)


def after(value, *others):
    return lax.optimization_barrier((value, *others))[0]


def exchange(axis, offset, size=4):
    return lambda value: lax.ppermute(value, axis, [(i, i ^ offset) for i in range(size)])


CORE, CHIP = exchange("row", 1), exchange("row", 2)
NEAR, FAR, OPPOSITE = exchange("col", 1), exchange("col", 2), exchange("col", 3)


def middle(value):
    return lax.ppermute(value, "col", MIDDLE)


def diagonal(value):
    return lax.ppermute(value, ("row", "col"), [(4 * r + c, 4 * (r ^ 2) + 3 - c) for r in range(4) for c in (1, 2)])


MIDDLE = [(1, 2), (2, 1)]


def local(corpus, sample_rows, initial):
    vecs, size = initial.shape
    half = size // 2
    count = 16
    total = float(size * count)
    scale = UNIT * UNIT / (2.0 * corpus.shape[1])
    levels = call(encode, [initial], jax.ShapeDtypeStruct((vecs // 2 + 8, size), jnp.int32))
    landmarks = lax.gather(
        corpus,
        sample_rows[:, None],
        lax.GatherDimensionNumbers(offset_dims=(1,), collapsed_slice_dims=(0,), start_index_map=(0,)),
        (1, corpus.shape[1]),
        mode="promise_in_bounds",
    )
    code = jnp.round(landmarks * (1.0 / UNIT)).astype(jnp.int32)
    own = jnp.concatenate([pair(code[:half], code[half:]), levels], axis=0)

    def build(*blocks):
        shapes = jax.ShapeDtypeStruct((len(blocks) * size, 2 * size), BF16), jax.ShapeDtypeStruct((vecs, len(blocks) * size), F32)
        tile, start = call(functools.partial(build_kernel, half, scale), [*side, *blocks], shapes)
        tiles.append(tile)
        starts.append(start)

    outer, partner, chip = NEAR(own), middle(own), CHIP(own)
    tiles, starts = [], []
    groups = [[own, outer, CORE(own), CORE(outer)]]
    codes = jax.ShapeDtypeStruct((2 * size, corpus.shape[1]), BF16)
    side = call(functools.partial(side_kernel, half, scale), [own, outer], (codes, codes, jax.ShapeDtypeStruct((1, 2 * size), F32)))
    build(*groups[0])
    partner_outer, chip_outer, chip_partner = middle(outer), NEAR(chip), CHIP(partner)
    groups.append([partner, CORE(partner), chip, CORE(chip)])
    build(*groups[1])
    chip_partner_outer = CHIP(after(partner_outer, tiles[0]))
    build(partner_outer, CORE(partner_outer))
    build(chip_partner, CORE(chip_partner))
    final = CORE(after(chip_partner_outer, *tiles[1:3]))
    build(chip_outer, CORE(chip_outer))
    build(chip_partner_outer)
    images, tile = call(
        functools.partial(first_kernel, len(tiles), half, scale, total),
        [*side, final, *tiles, *starts],
        (jax.ShapeDtypeStruct((vecs, 2 * size), F32), jax.ShapeDtypeStruct((size, 2 * size), BF16)),
    )
    tiles.append(tile)
    places = [images, middle(images), CHIP(images), diagonal(images)]
    pairs = [[value, CORE(value)] for value in places]
    block = jax.ShapeDtypeStruct((vecs, size), F32)
    parts = []
    for group in ([0, 1, 2],):
        values = [value for p in group for value in pairs[p]]
        shapes = jax.ShapeDtypeStruct((3 * vecs, len(values) * 2 * size), BF16), jax.ShapeDtypeStruct((vecs, vecs), F32)
        parts.append(call(functools.partial(partial_kernel, len(values)), [images, *values], (*shapes, jax.ShapeDtypeStruct((vecs, 128), F32))))
    here, part, chip, far = (4 * p for p in range(4))
    pieces = [here, here + 1, here + 2, here + 3, part, part + 2, chip, chip + 2]
    pieces += [part + 1, part + 3, far, far + 2, chip + 1, chip + 3, far + 1, far + 3]
    packed = jax.ShapeDtypeStruct((vecs // 2 + 8, 2 * vecs), F32)
    known = [part[i] for i in range(3) for part in parts]
    images, other, share = call(
        functools.partial(second_kernel, len(parts), pieces, total), [images, *pairs[3], *known, *tiles], (block, block, packed)
    )
    given = NEAR(other)
    place = lax.axis_index("col")
    flag = ((place == 0) | (place == 3)).astype(jnp.int32).reshape(1)
    share = call(functools.partial(merge_kernel, 2.0 * size), [share, CORE(share)], packed)
    smem = pl.BlockSpec(memory_space=pltpu.SMEM)
    share = call(
        functools.partial(column_kernel, 4.0 * size),
        [flag, share, NEAR(share), FAR(share), middle(share)],
        packed,
        [smem] + [VMEM] * 4,
    )
    return call(functools.partial(last_kernel, total), [flag, share, CHIP(share), images, given], block, [smem] + [VMEM] * 4)


def local_large(corpus, sample_rows, initial):
    both = ("row", "col")
    landmarks = corpus[sample_rows]
    everyone = lax.all_gather(landmarks, both, axis=0, tiled=True)
    total = float(everyone.shape[0])
    norms = jnp.sum(everyone * everyone, axis=1)
    own_norms = jnp.sum(landmarks * landmarks, axis=1)
    products = jnp.dot(everyone, landmarks.T, precision=HIGHEST, preferred_element_type=F32)
    tile = jnp.exp(-(norms[:, None] + own_norms[None, :] - 2.0 * products) / (2.0 * corpus.shape[1])).astype(BF16)
    starts = lax.all_gather(initial, both, axis=1, tiled=True)
    rounded = (starts - jnp.mean(starts, axis=1, keepdims=True)).astype(BF16)
    vectors = None
    for _ in range(ITERS):
        images = jnp.dot(rounded, tile, preferred_element_type=F32)
        gathered = lax.all_gather(images, both, axis=1, tiled=True)
        mean = jnp.mean(gathered, axis=1, keepdims=True)
        centered = gathered - mean
        factor = jnp.linalg.cholesky(jnp.dot(centered, centered.T, precision=HIGHEST))
        rounded = (math.sqrt(total) * jax.scipy.linalg.solve_triangular(factor, centered, lower=True)).astype(BF16)
        vectors = math.sqrt(total) * jax.scipy.linalg.solve_triangular(factor, images - mean, lower=True)
    return vectors


def solution(mesh):
    shape = mesh.shape
    whole = P(("groups", "row", "col"))
    return jax.shard_map(
        local if (shape["row"], shape["col"]) == (4, 4) else local_large,
        mesh=mesh,
        in_specs=(P(("groups", "row", "col"), None), whole, P(None, ("groups", "row", "col"))),
        out_specs=P(None, ("groups", "row", "col")),
        check_vma=False,
    )
```

```python
import functools
import math

import jax
import jax.numpy as jnp
from jax import lax
from jax.experimental import pallas as pl
from jax.experimental.pallas import tpu as pltpu
from jax.sharding import PartitionSpec as P

ITERS = 2
REACH = 20.0
UNIT = REACH / 32767.0
FIXED, RANGE = 2.0**28, 2.0**26
HIGHEST = lax.Precision.HIGHEST
BF16, F32 = jnp.bfloat16, jnp.float32
VMEM = pl.BlockSpec(memory_space=pltpu.VMEM)


def matmul(a, b, contract, precision=None):
    return lax.dot_general(a, b, ((contract[:1], contract[1:]), ((), ())), precision=precision, preferred_element_type=F32)


def pair(high, low):
    return (high << 16) | (low & 0xFFFF)


def unpair(words):
    return words >> 16, (words << 16) >> 16


def encode(initial_ref, out_ref):
    initial = initial_ref[...]
    vecs, size = initial.shape
    half = size // 2
    mean = jnp.round(jnp.sum(initial, axis=1, keepdims=True) * (FIXED / size)).astype(jnp.int32)
    apart = initial - mean.astype(F32) * (1.0 / FIXED)
    reach = jnp.ceil(jnp.max(jnp.abs(apart), axis=1, keepdims=True) * RANGE).astype(jnp.int32) + 1
    step = reach.astype(F32) * (1.0 / (RANGE * 32767.0))
    level = jnp.round(apart / step).astype(jnp.int32)
    words = pair(level[:, :half], level[:, half:])
    row = lax.broadcasted_iota(jnp.int32, (vecs, size), 0)
    lane = lax.broadcasted_iota(jnp.int32, (vecs, size), 1)
    header = jnp.where(lane == row, mean, jnp.where(lane == row + vecs, reach, 0))
    out_ref[: vecs // 2] = jnp.concatenate([words[: vecs // 2], words[vecs // 2 :]], axis=1)
    out_ref[vecs // 2 :] = jnp.broadcast_to(jnp.sum(header, axis=0, keepdims=True), (8, size))


def decode(block, half):
    words = block[half : block.shape[0] - 8]
    vecs = 2 * words.shape[0]
    level = jnp.concatenate([jnp.concatenate(unpair(part), axis=1) for part in (words[:, :half], words[:, half:])], axis=0)
    header = block[block.shape[0] - 8 :].astype(F32)[:1, : 2 * vecs]
    row = lax.broadcasted_iota(jnp.int32, (vecs, 2 * vecs), 0)
    lane = lax.broadcasted_iota(jnp.int32, (vecs, 2 * vecs), 1)
    mean = jnp.sum(jnp.where(lane == row, header, 0.0), axis=1, keepdims=True) * (1.0 / FIXED)
    step = jnp.sum(jnp.where(lane == row + vecs, header, 0.0), axis=1, keepdims=True) * (1.0 / (RANGE * 32767.0))
    return level.astype(F32) * step + mean


def split_codes(words):
    code = jnp.concatenate(unpair(words), axis=0)
    high = ((code + 128) >> 8) << 8
    return high.astype(F32).astype(BF16), (code - high).astype(F32).astype(BF16)


def kernel_rows(words, own_high, own_low, own_norms, scale):
    high, low = split_codes(words)
    wide = high.astype(F32) + low.astype(F32)
    norms = scale * jnp.sum(wide * wide, axis=1, keepdims=True)
    dots = matmul(high, own_high, (1, 1)) + (matmul(high, own_low, (1, 1)) + matmul(low, own_high, (1, 1))) + matmul(low, own_low, (1, 1))
    return jnp.exp((2.0 * scale) * dots - (norms + own_norms)).astype(BF16)


def own_side(refs, half, scale):
    parts = [split_codes(ref[:half]) for ref in refs]
    high = jnp.concatenate([part[0] for part in parts], axis=0)
    low = jnp.concatenate([part[1] for part in parts], axis=0)
    wide = high.astype(F32) + low.astype(F32)
    norms = matmul(jnp.ones((8, wide.shape[1]), F32), wide * wide, (1, 1), HIGHEST)[:1]
    return high, low, scale * norms


def side_kernel(half, scale, own_ref, outer_ref, high_ref, low_ref, norms_ref):
    high_ref[...], low_ref[...], norms_ref[...] = own_side((own_ref, outer_ref), half, scale)


def build_kernel(half, scale, *refs):
    side, blocks, (tile_ref, start_ref) = refs[:3], refs[3:-2], refs[-2:]
    for b, block in enumerate(blocks):
        place = pl.ds(b * 2 * half, 2 * half)
        tile_ref[place, :] = kernel_rows(block[:half], *(ref[...] for ref in side), scale)
        start_ref[:, place] = decode(block[...], half)


def first_kernel(count, half, scale, total, *refs):
    side, block, tiles, parts = refs[:3], refs[3], refs[4 : 4 + count], refs[4 + count : -2]
    out_ref, tile_ref = refs[-2:]
    size = 2 * half
    tile_ref[...] = kernel_rows(block[:half], *(ref[...] for ref in side), scale)
    starts = [part[...] for part in parts] + [decode(block[...], half)]
    pieces = [start[:, b : b + size] for start in starts for b in range(0, start.shape[1], size)]
    sums = pieces[0]
    for piece in pieces[1:]:
        sums = sums + piece
    mean = jnp.sum(sums, axis=1, keepdims=True) / total
    images = None
    for start, tile in zip(starts, (*tiles, tile_ref)):
        term = matmul((start - mean).astype(BF16), tile[...], (1, 0))
        images = term if images is None else images + term
    out_ref[...] = images


def inverse_factor(gram):
    n = gram.shape[0]
    row_id = lax.broadcasted_iota(jnp.int32, (n, 2 * n), 0)
    col_id = lax.broadcasted_iota(jnp.int32, (n, 2 * n), 1)
    eye = (row_id[:, :n] == col_id[:, :n]).astype(F32)
    work = jnp.concatenate([gram, eye], axis=1)
    done = []
    for top in range(0, n, 8):
        rows = n - top
        place = lax.broadcasted_iota(jnp.int32, (rows, 2 * n), 0)
        columns = [jnp.broadcast_to(work[:, top + k : top + k + 1], (rows, 2 * n)) for k in range(8)]
        for k in range(0, 8, 2):
            one, two = columns[k], columns[k + 1]
            a, b, d = one[k : k + 1], one[k + 1 : k + 2], two[k + 1 : k + 2]
            inverse = 1.0 / a
            slope = b * inverse
            second = jnp.where(place > k + 1, (two * a - one * b) * (1.0 / (a * d - b * b)), 0.0)
            first = jnp.where(place > k, one, 0.0)

            def eliminate(value):
                upper = value[k : k + 1]
                return value - first * (upper * inverse) - second * (value[k + 1 : k + 2] - slope * upper)

            work = eliminate(work)
            columns = columns[: k + 2] + [eliminate(column) for column in columns[k + 2 :]]
        done.append(work[:8])
        work = work[8:]
    upper = jnp.concatenate(done, axis=0)
    pivots = jnp.sum(jnp.where(row_id == col_id, upper, 0.0), axis=1, keepdims=True)
    return upper[:, n:] * lax.rsqrt(pivots)


def thirds(value):
    high = value.astype(BF16)
    rest = value - high.astype(F32)
    middle = rest.astype(BF16)
    return jnp.concatenate([high, middle, (rest - middle.astype(F32)).astype(BF16)], axis=0)


def gram_of(stack):
    n = stack.shape[0] // 3
    p = matmul(stack, stack, (1, 1))
    middle = p[n : 2 * n, n : 2 * n] + (p[:n, 2 * n :] + p[2 * n :, :n])
    return p[:n, :n] + ((p[:n, n : 2 * n] + p[n : 2 * n, :n]) + middle)


def times(matrix, stack):
    n = matrix.shape[0]
    parts = thirds(matrix)
    p = matmul(jnp.concatenate([parts, parts, parts], axis=1), stack, (1, 0))
    return p[:n] + (p[n : 2 * n] + p[2 * n :])


def partial_kernel(count, *refs):
    shift_ref, images = refs[0], refs[1 : 1 + count]
    stack_ref, gram_ref, sum_ref = refs[-3:]
    value = jnp.concatenate([image[...] for image in images], axis=1) - shift_of(shift_ref)
    stack = thirds(value)
    stack_ref[...] = stack
    gram_ref[...] = gram_of(stack)
    sum_ref[...] = jnp.broadcast_to(jnp.sum(value, axis=1, keepdims=True), sum_ref.shape)


def shift_of(ref):
    return jnp.sum(ref[...], axis=1, keepdims=True) * (1.0 / ref.shape[1])


def second_kernel(parts, pieces, total, *refs):
    shift_ref, images = refs[0], refs[1:3]
    stacks, grams, sums = (refs[3 + i * parts : 3 + (i + 1) * parts] for i in range(3))
    tiles = refs[3 + 3 * parts : -3]
    own_ref, other_ref, share_ref = refs[-3:]
    size = own_ref.shape[1]
    value = jnp.concatenate([image[...] for image in images], axis=1) - shift_of(shift_ref)
    stack = thirds(value)
    gram = gram_of(stack)
    far = jnp.sum(value, axis=1, keepdims=True)
    for part, sum_part in zip(grams, sums):
        gram, far = gram + part[...], far + sum_part[:, :1]
    far = far * (1.0 / total)
    n = gram.shape[0]
    eye = lax.broadcasted_iota(jnp.int32, (n, n), 0) == lax.broadcasted_iota(jnp.int32, (n, n), 1)
    gram = gram - (total * far) * jnp.sum(jnp.where(eye, far, 0.0), axis=0, keepdims=True)
    solve = math.sqrt(total) * inverse_factor(gram)
    level = times(solve, thirds(jnp.broadcast_to(far, (n, 2 * n))))[:, :1]
    vectors = []
    for part in (*stacks, None):
        whole = stack if part is None else part[...]
        vectors.append((times(solve, whole) - level).astype(BF16))
    vectors = jnp.concatenate(vectors, axis=1)
    vectors = jnp.concatenate([vectors[:, p * size : (p + 1) * size] for p in pieces], axis=1)
    result, begin = None, 0
    for tile in tiles:
        end = begin + tile.shape[0]
        term = matmul(vectors[:, begin:end], tile[...], (1, 0))
        result, begin = term if result is None else result + term, end
    own_ref[...] = result[:, :size]
    other_ref[...] = result[:, size:]
    local_mean = jnp.sum(result, axis=1, keepdims=True) / (2 * size)
    gram = gram_of(thirds(result - local_mean))
    h = n // 2
    across = jnp.sum(jnp.where(eye, local_mean, 0.0), axis=0, keepdims=True)
    share_ref[:h] = jnp.concatenate([gram[:h], gram[h:, h:], local_mean[:h], local_mean[h:], jnp.zeros((h, h - 2), F32)], axis=1)
    share_ref[h:] = jnp.broadcast_to(jnp.concatenate([across, across[:, h:], jnp.zeros((1, h), F32)], axis=1), (8, 4 * h))


def merge(a, b, each):
    h = a.shape[0] - 8
    apart = a - b
    lane = lax.broadcasted_iota(jnp.int32, (h, 4 * h), 1)
    down = jnp.where(lane < 2 * h, apart[:h, 3 * h : 3 * h + 1], apart[:h, 3 * h + 1 : 3 * h + 2])
    both = a + b
    top = jnp.where(lane < 3 * h, both[:h] + (0.5 * each) * (down * apart[h : h + 1]), 0.5 * both[:h])
    return jnp.concatenate([top, 0.5 * both[h:]], axis=0)


def merge_kernel(each, a_ref, b_ref, out_ref):
    out_ref[...] = merge(a_ref[...], b_ref[...], each)


def column_kernel(each, outer_ref, share_ref, near_ref, far_ref, across_ref, out_ref):
    outer = outer_ref[0] == 1
    first = jnp.where(outer, near_ref[...], share_ref[...])
    out_ref[...] = merge(first, jnp.where(outer, far_ref[...], across_ref[...]), each)


def last_kernel(total, outer_ref, share_ref, beside_ref, own_ref, given_ref, out_ref):
    images = jnp.where(outer_ref[0] == 1, given_ref[...], own_ref[...])
    share = merge(share_ref[...], beside_ref[...], 0.5 * total)
    h = share.shape[0] - 8
    mean = jnp.concatenate([share[:h, 3 * h : 3 * h + 1], share[:h, 3 * h + 1 : 3 * h + 2]], axis=0)
    top = share[:h, : 2 * h]
    bottom = jnp.concatenate([top[:, h:].T, share[:h, 2 * h : 3 * h]], axis=1)
    solve = math.sqrt(total) * inverse_factor(jnp.concatenate([top, bottom], axis=0))
    out_ref[...] = times(solve, thirds(images - mean))


def call(kernel, args, out_shape, in_specs=None):
    return pl.pallas_call(
        kernel,
        out_shape=out_shape,
        in_specs=in_specs or [VMEM] * len(args),
        out_specs=jax.tree.map(lambda _: VMEM, out_shape),
        compiler_params=pltpu.CompilerParams(vmem_limit_bytes=24 * 2**20),
    )(*args)


def after(value, *others):
    return lax.optimization_barrier((value, *others))[0]


def exchange(axis, offset, size=4):
    return lambda value: lax.ppermute(value, axis, [(i, i ^ offset) for i in range(size)])


CORE, CHIP = exchange("row", 1), exchange("row", 2)
NEAR, FAR, OPPOSITE = exchange("col", 1), exchange("col", 2), exchange("col", 3)


def middle(value):
    return lax.ppermute(value, ("row", "col"), [(4 * r + c, 4 * (r ^ 0) + 3 - c) if c in (1, 2) else (4 * r + c, 4 * (r ^ 1) + c) for r in range(4) for c in range(4)])


def diagonal(value):
    return lax.ppermute(value, ("row", "col"), [(4 * r + c, 4 * (r ^ 2) + 3 - c) if c in (1, 2) else (4 * r + c, 4 * (r ^ 1) + c) for r in range(4) for c in range(4)])


MIDDLE = [(1, 2), (2, 1)]


def local(corpus, sample_rows, initial):
    vecs, size = initial.shape
    half = size // 2
    count = 16
    total = float(size * count)
    scale = UNIT * UNIT / (2.0 * corpus.shape[1])
    levels = call(encode, [initial], jax.ShapeDtypeStruct((vecs // 2 + 8, size), jnp.int32))
    landmarks = lax.gather(
        corpus,
        sample_rows[:, None],
        lax.GatherDimensionNumbers(offset_dims=(1,), collapsed_slice_dims=(0,), start_index_map=(0,)),
        (1, corpus.shape[1]),
        mode="promise_in_bounds",
    )
    code = jnp.round(landmarks * (1.0 / UNIT)).astype(jnp.int32)
    own = jnp.concatenate([pair(code[:half], code[half:]), levels], axis=0)

    def build(*blocks):
        shapes = jax.ShapeDtypeStruct((len(blocks) * size, 2 * size), BF16), jax.ShapeDtypeStruct((vecs, len(blocks) * size), F32)
        tile, start = call(functools.partial(build_kernel, half, scale), [*side, *blocks], shapes)
        tiles.append(tile)
        starts.append(start)

    outer, partner, chip = NEAR(own), middle(own), CHIP(own)
    tiles, starts = [], []
    groups = [[own, outer, CORE(own), CORE(outer)]]
    codes = jax.ShapeDtypeStruct((2 * size, corpus.shape[1]), BF16)
    side = call(functools.partial(side_kernel, half, scale), [own, outer], (codes, codes, jax.ShapeDtypeStruct((1, 2 * size), F32)))
    build(*groups[0])
    partner_outer, chip_outer, chip_partner = middle(outer), NEAR(chip), CHIP(partner)
    groups.append([partner, CORE(partner), chip, CORE(chip)])
    build(*groups[1])
    chip_partner_outer = CHIP(after(partner_outer, tiles[0]))
    build(partner_outer, CORE(partner_outer))
    build(chip_partner, CORE(chip_partner))
    final = CORE(after(chip_partner_outer, *tiles[1:3]))
    build(chip_outer, CORE(chip_outer))
    build(chip_partner_outer)
    images, tile = call(
        functools.partial(first_kernel, len(tiles), half, scale, total),
        [*side, final, *tiles, *starts],
        (jax.ShapeDtypeStruct((vecs, 2 * size), F32), jax.ShapeDtypeStruct((size, 2 * size), BF16)),
    )
    tiles.append(tile)
    places = [images, middle(images), CHIP(images), diagonal(images)]
    pairs = [[value, CORE(value)] for value in places]
    block = jax.ShapeDtypeStruct((vecs, size), F32)
    parts = []
    for group in ([0, 1, 2],):
        values = [value for p in group for value in pairs[p]]
        shapes = jax.ShapeDtypeStruct((3 * vecs, len(values) * 2 * size), BF16), jax.ShapeDtypeStruct((vecs, vecs), F32)
        parts.append(call(functools.partial(partial_kernel, len(values)), [images, *values], (*shapes, jax.ShapeDtypeStruct((vecs, 128), F32))))
    here, part, chip, far = (4 * p for p in range(4))
    pieces = [here, here + 1, here + 2, here + 3, part, part + 2, chip, chip + 2]
    pieces += [part + 1, part + 3, far, far + 2, chip + 1, chip + 3, far + 1, far + 3]
    packed = jax.ShapeDtypeStruct((vecs // 2 + 8, 2 * vecs), F32)
    known = [part[i] for i in range(3) for part in parts]
    images, other, share = call(
        functools.partial(second_kernel, len(parts), pieces, total), [images, *pairs[3], *known, *tiles], (block, block, packed)
    )
    given = NEAR(other)
    place = lax.axis_index("col")
    flag = ((place == 0) | (place == 3)).astype(jnp.int32).reshape(1)
    share = call(functools.partial(merge_kernel, 2.0 * size), [share, CORE(share)], packed)
    smem = pl.BlockSpec(memory_space=pltpu.SMEM)
    share = call(
        functools.partial(column_kernel, 4.0 * size),
        [flag, share, NEAR(share), FAR(share), middle(share)],
        packed,
        [smem] + [VMEM] * 4,
    )
    return call(functools.partial(last_kernel, total), [flag, share, CHIP(share), images, given], block, [smem] + [VMEM] * 4)


def local_large(corpus, sample_rows, initial):
    both = ("row", "col")
    landmarks = corpus[sample_rows]
    everyone = lax.all_gather(landmarks, both, axis=0, tiled=True)
    total = float(everyone.shape[0])
    norms = jnp.sum(everyone * everyone, axis=1)
    own_norms = jnp.sum(landmarks * landmarks, axis=1)
    products = jnp.dot(everyone, landmarks.T, precision=HIGHEST, preferred_element_type=F32)
    tile = jnp.exp(-(norms[:, None] + own_norms[None, :] - 2.0 * products) / (2.0 * corpus.shape[1])).astype(BF16)
    starts = lax.all_gather(initial, both, axis=1, tiled=True)
    rounded = (starts - jnp.mean(starts, axis=1, keepdims=True)).astype(BF16)
    vectors = None
    for _ in range(ITERS):
        images = jnp.dot(rounded, tile, preferred_element_type=F32)
        gathered = lax.all_gather(images, both, axis=1, tiled=True)
        mean = jnp.mean(gathered, axis=1, keepdims=True)
        centered = gathered - mean
        factor = jnp.linalg.cholesky(jnp.dot(centered, centered.T, precision=HIGHEST))
        rounded = (math.sqrt(total) * jax.scipy.linalg.solve_triangular(factor, centered, lower=True)).astype(BF16)
        vectors = math.sqrt(total) * jax.scipy.linalg.solve_triangular(factor, images - mean, lower=True)
    return vectors


def solution(mesh):
    shape = mesh.shape
    whole = P(("groups", "row", "col"))
    return jax.shard_map(
        local if (shape["row"], shape["col"]) == (4, 4) else local_large,
        mesh=mesh,
        in_specs=(P(("groups", "row", "col"), None), whole, P(None, ("groups", "row", "col"))),
        out_specs=P(None, ("groups", "row", "col")),
        check_vma=False,
    )
```

```python
import functools
import math

import jax
import jax.numpy as jnp
from jax import lax
from jax.experimental import pallas as pl
from jax.experimental.pallas import tpu as pltpu
from jax.sharding import PartitionSpec as P

ITERS = 2
REACH = 20.0
UNIT = REACH / 32767.0
FIXED, RANGE = 2.0**28, 2.0**26
HIGHEST = lax.Precision.HIGHEST
BF16, F32 = jnp.bfloat16, jnp.float32
VMEM = pl.BlockSpec(memory_space=pltpu.VMEM)


def matmul(a, b, contract, precision=None):
    return lax.dot_general(a, b, ((contract[:1], contract[1:]), ((), ())), precision=precision, preferred_element_type=F32)


def pair(high, low):
    return (high << 16) | (low & 0xFFFF)


def unpair(words):
    return words >> 16, (words << 16) >> 16


def encode(initial_ref, out_ref):
    initial = initial_ref[...]
    vecs, size = initial.shape
    half = size // 2
    mean = jnp.round(jnp.sum(initial, axis=1, keepdims=True) * (FIXED / size)).astype(jnp.int32)
    apart = initial - mean.astype(F32) * (1.0 / FIXED)
    reach = jnp.ceil(jnp.max(jnp.abs(apart), axis=1, keepdims=True) * RANGE).astype(jnp.int32) + 1
    step = reach.astype(F32) * (1.0 / (RANGE * 32767.0))
    level = jnp.round(apart / step).astype(jnp.int32)
    words = pair(level[:, :half], level[:, half:])
    row = lax.broadcasted_iota(jnp.int32, (vecs, size), 0)
    lane = lax.broadcasted_iota(jnp.int32, (vecs, size), 1)
    header = jnp.where(lane == row, mean, jnp.where(lane == row + vecs, reach, 0))
    out_ref[: vecs // 2] = jnp.concatenate([words[: vecs // 2], words[vecs // 2 :]], axis=1)
    out_ref[vecs // 2 :] = jnp.broadcast_to(jnp.sum(header, axis=0, keepdims=True), (8, size))


def decode(block, half):
    words = block[half : block.shape[0] - 8]
    vecs = 2 * words.shape[0]
    level = jnp.concatenate([jnp.concatenate(unpair(part), axis=1) for part in (words[:, :half], words[:, half:])], axis=0)
    header = block[block.shape[0] - 8 :].astype(F32)[:1, : 2 * vecs]
    row = lax.broadcasted_iota(jnp.int32, (vecs, 2 * vecs), 0)
    lane = lax.broadcasted_iota(jnp.int32, (vecs, 2 * vecs), 1)
    mean = jnp.sum(jnp.where(lane == row, header, 0.0), axis=1, keepdims=True) * (1.0 / FIXED)
    step = jnp.sum(jnp.where(lane == row + vecs, header, 0.0), axis=1, keepdims=True) * (1.0 / (RANGE * 32767.0))
    return level.astype(F32) * step + mean


def split_codes(words):
    code = jnp.concatenate(unpair(words), axis=0)
    high = ((code + 128) >> 8) << 8
    return high.astype(F32).astype(BF16), (code - high).astype(F32).astype(BF16)


def kernel_rows(words, own_high, own_low, own_norms, scale):
    high, low = split_codes(words)
    wide = high.astype(F32) + low.astype(F32)
    norms = scale * jnp.sum(wide * wide, axis=1, keepdims=True)
    dots = matmul(high, own_high, (1, 1)) + (matmul(high, own_low, (1, 1)) + matmul(low, own_high, (1, 1))) + matmul(low, own_low, (1, 1))
    return jnp.exp((2.0 * scale) * dots - (norms + own_norms)).astype(BF16)


def own_side(refs, half, scale):
    parts = [split_codes(ref[:half]) for ref in refs]
    high = jnp.concatenate([part[0] for part in parts], axis=0)
    low = jnp.concatenate([part[1] for part in parts], axis=0)
    wide = high.astype(F32) + low.astype(F32)
    norms = matmul(jnp.ones((8, wide.shape[1]), F32), wide * wide, (1, 1), HIGHEST)[:1]
    return high, low, scale * norms


def side_kernel(half, scale, own_ref, outer_ref, high_ref, low_ref, norms_ref):
    high_ref[...], low_ref[...], norms_ref[...] = own_side((own_ref, outer_ref), half, scale)


def build_kernel(half, scale, *refs):
    side, blocks, (tile_ref, start_ref) = refs[:3], refs[3:-2], refs[-2:]
    for b, block in enumerate(blocks):
        place = pl.ds(b * 2 * half, 2 * half)
        tile_ref[place, :] = kernel_rows(block[:half], *(ref[...] for ref in side), scale)
        start_ref[:, place] = decode(block[...], half)


def first_kernel(count, half, scale, total, *refs):
    side, block, tiles, parts = refs[:3], refs[3], refs[4 : 4 + count], refs[4 + count : -2]
    out_ref, tile_ref = refs[-2:]
    size = 2 * half
    tile_ref[...] = kernel_rows(block[:half], *(ref[...] for ref in side), scale)
    starts = [part[...] for part in parts] + [decode(block[...], half)]
    pieces = [start[:, b : b + size] for start in starts for b in range(0, start.shape[1], size)]
    sums = pieces[0]
    for piece in pieces[1:]:
        sums = sums + piece
    mean = jnp.sum(sums, axis=1, keepdims=True) / total
    images = None
    for start, tile in zip(starts, (*tiles, tile_ref)):
        term = matmul((start - mean).astype(BF16), tile[...], (1, 0))
        images = term if images is None else images + term
    out_ref[...] = images


def inverse_factor(gram):
    n = gram.shape[0]
    row_id = lax.broadcasted_iota(jnp.int32, (n, 2 * n), 0)
    col_id = lax.broadcasted_iota(jnp.int32, (n, 2 * n), 1)
    eye = (row_id[:, :n] == col_id[:, :n]).astype(F32)
    work = jnp.concatenate([gram, eye], axis=1)
    done = []
    for top in range(0, n, 8):
        rows = n - top
        place = lax.broadcasted_iota(jnp.int32, (rows, 2 * n), 0)
        columns = [jnp.broadcast_to(work[:, top + k : top + k + 1], (rows, 2 * n)) for k in range(8)]
        for k in range(0, 8, 2):
            one, two = columns[k], columns[k + 1]
            a, b, d = one[k : k + 1], one[k + 1 : k + 2], two[k + 1 : k + 2]
            inverse = 1.0 / a
            slope = b * inverse
            second = jnp.where(place > k + 1, (two * a - one * b) * (1.0 / (a * d - b * b)), 0.0)
            first = jnp.where(place > k, one, 0.0)

            def eliminate(value):
                upper = value[k : k + 1]
                return value - first * (upper * inverse) - second * (value[k + 1 : k + 2] - slope * upper)

            work = eliminate(work)
            columns = columns[: k + 2] + [eliminate(column) for column in columns[k + 2 :]]
        done.append(work[:8])
        work = work[8:]
    upper = jnp.concatenate(done, axis=0)
    pivots = jnp.sum(jnp.where(row_id == col_id, upper, 0.0), axis=1, keepdims=True)
    return upper[:, n:] * lax.rsqrt(pivots)


def thirds(value):
    high = value.astype(BF16)
    rest = value - high.astype(F32)
    middle = rest.astype(BF16)
    return jnp.concatenate([high, middle, (rest - middle.astype(F32)).astype(BF16)], axis=0)


def gram_of(stack):
    n = stack.shape[0] // 3
    p = matmul(stack, stack, (1, 1))
    middle = p[n : 2 * n, n : 2 * n] + (p[:n, 2 * n :] + p[2 * n :, :n])
    return p[:n, :n] + ((p[:n, n : 2 * n] + p[n : 2 * n, :n]) + middle)


def times(matrix, stack):
    n = matrix.shape[0]
    parts = thirds(matrix)
    p = matmul(jnp.concatenate([parts, parts, parts], axis=1), stack, (1, 0))
    return p[:n] + (p[n : 2 * n] + p[2 * n :])


def partial_kernel(count, *refs):
    shift_ref, images = refs[0], refs[1 : 1 + count]
    stack_ref, gram_ref, sum_ref = refs[-3:]
    value = jnp.concatenate([image[...] for image in images], axis=1) - shift_of(shift_ref)
    stack = thirds(value)
    stack_ref[...] = stack
    gram_ref[...] = gram_of(stack)
    sum_ref[...] = jnp.broadcast_to(jnp.sum(value, axis=1, keepdims=True), sum_ref.shape)


def shift_of(ref):
    return jnp.sum(ref[...], axis=1, keepdims=True) * (1.0 / ref.shape[1])


def second_kernel(parts, pieces, total, *refs):
    shift_ref, images = refs[0], refs[1:3]
    stacks, grams, sums = (refs[3 + i * parts : 3 + (i + 1) * parts] for i in range(3))
    tiles = refs[3 + 3 * parts : -3]
    own_ref, other_ref, share_ref = refs[-3:]
    size = own_ref.shape[1]
    value = jnp.concatenate([image[...] for image in images], axis=1) - shift_of(shift_ref)
    stack = thirds(value)
    gram = gram_of(stack)
    far = jnp.sum(value, axis=1, keepdims=True)
    for part, sum_part in zip(grams, sums):
        gram, far = gram + part[...], far + sum_part[:, :1]
    far = far * (1.0 / total)
    n = gram.shape[0]
    eye = lax.broadcasted_iota(jnp.int32, (n, n), 0) == lax.broadcasted_iota(jnp.int32, (n, n), 1)
    gram = gram - (total * far) * jnp.sum(jnp.where(eye, far, 0.0), axis=0, keepdims=True)
    solve = math.sqrt(total) * inverse_factor(gram)
    level = times(solve, thirds(jnp.broadcast_to(far, (n, 2 * n))))[:, :1]
    vectors = []
    for part in (*stacks, None):
        whole = stack if part is None else part[...]
        vectors.append((times(solve, whole) - level).astype(BF16))
    vectors = jnp.concatenate(vectors, axis=1)
    vectors = jnp.concatenate([vectors[:, p * size : (p + 1) * size] for p in pieces], axis=1)
    result, begin = None, 0
    for tile in tiles:
        end = begin + tile.shape[0]
        term = matmul(vectors[:, begin:end], tile[...], (1, 0))
        result, begin = term if result is None else result + term, end
    own_ref[...] = result[:, :size]
    other_ref[...] = result[:, size:]
    local_mean = jnp.sum(result, axis=1, keepdims=True) / (2 * size)
    gram = gram_of(thirds(result - local_mean))
    h = n // 2
    across = jnp.sum(jnp.where(eye, local_mean, 0.0), axis=0, keepdims=True)
    share_ref[:h] = jnp.concatenate([gram[:h], gram[h:, h:], local_mean[:h], local_mean[h:], jnp.zeros((h, h - 2), F32)], axis=1)
    share_ref[h:] = jnp.broadcast_to(jnp.concatenate([across, across[:, h:], jnp.zeros((1, h), F32)], axis=1), (8, 4 * h))


def merge(a, b, each):
    h = a.shape[0] - 8
    apart = a - b
    lane = lax.broadcasted_iota(jnp.int32, (h, 4 * h), 1)
    down = jnp.where(lane < 2 * h, apart[:h, 3 * h : 3 * h + 1], apart[:h, 3 * h + 1 : 3 * h + 2])
    both = a + b
    top = jnp.where(lane < 3 * h, both[:h] + (0.5 * each) * (down * apart[h : h + 1]), 0.5 * both[:h])
    return jnp.concatenate([top, 0.5 * both[h:]], axis=0)


def merge_kernel(each, a_ref, b_ref, out_ref):
    out_ref[...] = merge(a_ref[...], b_ref[...], each)


def column_kernel(each, outer_ref, share_ref, near_ref, far_ref, across_ref, out_ref):
    outer = outer_ref[0] == 1
    first = jnp.where(outer, near_ref[...], share_ref[...])
    out_ref[...] = merge(first, jnp.where(outer, far_ref[...], across_ref[...]), each)


def last_kernel(total, outer_ref, share_ref, beside_ref, own_ref, given_ref, out_ref):
    images = jnp.where(outer_ref[0] == 1, given_ref[...], own_ref[...])
    share = merge(share_ref[...], beside_ref[...], 0.5 * total)
    h = share.shape[0] - 8
    mean = jnp.concatenate([share[:h, 3 * h : 3 * h + 1], share[:h, 3 * h + 1 : 3 * h + 2]], axis=0)
    top = share[:h, : 2 * h]
    bottom = jnp.concatenate([top[:, h:].T, share[:h, 2 * h : 3 * h]], axis=1)
    solve = math.sqrt(total) * inverse_factor(jnp.concatenate([top, bottom], axis=0))
    out_ref[...] = times(solve, thirds(images - mean))


def call(kernel, args, out_shape, in_specs=None):
    return pl.pallas_call(
        kernel,
        out_shape=out_shape,
        in_specs=in_specs or [VMEM] * len(args),
        out_specs=jax.tree.map(lambda _: VMEM, out_shape),
        compiler_params=pltpu.CompilerParams(vmem_limit_bytes=24 * 2**20),
    )(*args)


def after(value, *others):
    return lax.optimization_barrier((value, *others))[0]


def exchange(axis, offset, size=4):
    return lambda value: lax.ppermute(value, axis, [(i, i ^ offset) for i in range(size)])


CORE, CHIP = exchange("row", 1), exchange("row", 2)
NEAR, FAR, OPPOSITE = exchange("col", 1), exchange("col", 2), exchange("col", 3)


def middle(value):
    return lax.ppermute(value, ("row", "col"), [(4 * r + c, 4 * (r ^ 0) + 3 - c) if c in (1, 2) else (4 * r + c, 4 * (r ^ 1) + c) for r in range(4) for c in range(4)])


def diagonal(value):
    return lax.ppermute(value, ("row", "col"), [(4 * r + c, 4 * (r ^ 2) + 3 - c) if c in (1, 2) else (4 * r + c, 4 * (r ^ 1) + c) for r in range(4) for c in range(4)])


MIDDLE = [(1, 2), (2, 1)]


def local(corpus, sample_rows, initial):
    vecs, size = initial.shape
    half = size // 2
    count = 16
    total = float(size * count)
    scale = UNIT * UNIT / (2.0 * corpus.shape[1])
    levels = call(encode, [initial], jax.ShapeDtypeStruct((vecs // 2 + 8, size), jnp.int32))
    landmarks = lax.gather(
        corpus,
        sample_rows[:, None],
        lax.GatherDimensionNumbers(offset_dims=(1,), collapsed_slice_dims=(0,), start_index_map=(0,)),
        (1, corpus.shape[1]),
        mode="promise_in_bounds",
    )
    code = jnp.round(landmarks * (1.0 / UNIT)).astype(jnp.int32)
    own = jnp.concatenate([pair(code[:half], code[half:]), levels], axis=0)

    def build(*blocks):
        shapes = jax.ShapeDtypeStruct((len(blocks) * size, 2 * size), BF16), jax.ShapeDtypeStruct((vecs, len(blocks) * size), F32)
        tile, start = call(functools.partial(build_kernel, half, scale), [*side, *blocks], shapes)
        tiles.append(tile)
        starts.append(start)

    outer, partner, chip = NEAR(own), middle(own), CHIP(own)
    tiles, starts = [], []
    groups = [[own, outer, CORE(own), CORE(outer)]]
    codes = jax.ShapeDtypeStruct((2 * size, corpus.shape[1]), BF16)
    side = call(functools.partial(side_kernel, half, scale), [own, outer], (codes, codes, jax.ShapeDtypeStruct((1, 2 * size), F32)))
    build(*groups[0])
    partner_outer, chip_outer, chip_partner = middle(outer), NEAR(chip), CHIP(partner)
    groups.append([partner, CORE(partner), chip, CORE(chip)])
    build(*groups[1])
    chip_partner_outer = CHIP(after(partner_outer, tiles[0]))
    build(partner_outer, CORE(partner_outer))
    build(chip_partner, CORE(chip_partner))
    final = CORE(after(chip_partner_outer, *tiles[1:5]))
    build(chip_outer, CORE(chip_outer))
    build(chip_partner_outer)
    images, tile = call(
        functools.partial(first_kernel, len(tiles), half, scale, total),
        [*side, final, *tiles, *starts],
        (jax.ShapeDtypeStruct((vecs, 2 * size), F32), jax.ShapeDtypeStruct((size, 2 * size), BF16)),
    )
    tiles.append(tile)
    places = [images, middle(images), CHIP(images), diagonal(images)]
    pairs = [[value, CORE(value)] for value in places]
    block = jax.ShapeDtypeStruct((vecs, size), F32)
    parts = []
    for group in ([0, 1, 2],):
        values = [value for p in group for value in pairs[p]]
        shapes = jax.ShapeDtypeStruct((3 * vecs, len(values) * 2 * size), BF16), jax.ShapeDtypeStruct((vecs, vecs), F32)
        parts.append(call(functools.partial(partial_kernel, len(values)), [images, *values], (*shapes, jax.ShapeDtypeStruct((vecs, 128), F32))))
    here, part, chip, far = (4 * p for p in range(4))
    pieces = [here, here + 1, here + 2, here + 3, part, part + 2, chip, chip + 2]
    pieces += [part + 1, part + 3, far, far + 2, chip + 1, chip + 3, far + 1, far + 3]
    packed = jax.ShapeDtypeStruct((vecs // 2 + 8, 2 * vecs), F32)
    known = [part[i] for i in range(3) for part in parts]
    images, other, share = call(
        functools.partial(second_kernel, len(parts), pieces, total), [images, *pairs[3], *known, *tiles], (block, block, packed)
    )
    given = NEAR(other)
    place = lax.axis_index("col")
    flag = ((place == 0) | (place == 3)).astype(jnp.int32).reshape(1)
    share = call(functools.partial(merge_kernel, 2.0 * size), [share, CORE(share)], packed)
    smem = pl.BlockSpec(memory_space=pltpu.SMEM)
    share = call(
        functools.partial(column_kernel, 4.0 * size),
        [flag, share, NEAR(share), lax.ppermute(share, "col", [(0, 1), (1, 3), (2, 0), (3, 2)]), middle(share)],
        packed,
        [smem] + [VMEM] * 4,
    )
    return call(functools.partial(last_kernel, total), [flag, share, CHIP(share), images, given], block, [smem] + [VMEM] * 4)


def local_large(corpus, sample_rows, initial):
    both = ("row", "col")
    landmarks = corpus[sample_rows]
    everyone = lax.all_gather(landmarks, both, axis=0, tiled=True)
    total = float(everyone.shape[0])
    norms = jnp.sum(everyone * everyone, axis=1)
    own_norms = jnp.sum(landmarks * landmarks, axis=1)
    products = jnp.dot(everyone, landmarks.T, precision=HIGHEST, preferred_element_type=F32)
    tile = jnp.exp(-(norms[:, None] + own_norms[None, :] - 2.0 * products) / (2.0 * corpus.shape[1])).astype(BF16)
    starts = lax.all_gather(initial, both, axis=1, tiled=True)
    rounded = (starts - jnp.mean(starts, axis=1, keepdims=True)).astype(BF16)
    vectors = None
    for _ in range(ITERS):
        images = jnp.dot(rounded, tile, preferred_element_type=F32)
        gathered = lax.all_gather(images, both, axis=1, tiled=True)
        mean = jnp.mean(gathered, axis=1, keepdims=True)
        centered = gathered - mean
        factor = jnp.linalg.cholesky(jnp.dot(centered, centered.T, precision=HIGHEST))
        rounded = (math.sqrt(total) * jax.scipy.linalg.solve_triangular(factor, centered, lower=True)).astype(BF16)
        vectors = math.sqrt(total) * jax.scipy.linalg.solve_triangular(factor, images - mean, lower=True)
    return vectors


def solution(mesh):
    shape = mesh.shape
    whole = P(("groups", "row", "col"))
    return jax.shard_map(
        local if (shape["row"], shape["col"]) == (4, 4) else local_large,
        mesh=mesh,
        in_specs=(P(("groups", "row", "col"), None), whole, P(None, ("groups", "row", "col"))),
        out_specs=P(None, ("groups", "row", "col")),
        check_vma=False,
    )
```

```python
import functools
import math

import jax
import jax.numpy as jnp
from jax import lax
from jax.experimental import pallas as pl
from jax.experimental.pallas import tpu as pltpu
from jax.sharding import PartitionSpec as P

ITERS = 2
REACH = 20.0
UNIT = REACH / 32767.0
FIXED, RANGE = 2.0**28, 2.0**26
HIGHEST = lax.Precision.HIGHEST
BF16, F32 = jnp.bfloat16, jnp.float32
VMEM = pl.BlockSpec(memory_space=pltpu.VMEM)


def matmul(a, b, contract, precision=None):
    return lax.dot_general(a, b, ((contract[:1], contract[1:]), ((), ())), precision=precision, preferred_element_type=F32)


def pair(high, low):
    return (high << 16) | (low & 0xFFFF)


def unpair(words):
    return words >> 16, (words << 16) >> 16


def encode(initial_ref, out_ref):
    initial = initial_ref[...]
    vecs, size = initial.shape
    half = size // 2
    mean = jnp.round(jnp.sum(initial, axis=1, keepdims=True) * (FIXED / size)).astype(jnp.int32)
    apart = initial - mean.astype(F32) * (1.0 / FIXED)
    reach = jnp.ceil(jnp.max(jnp.abs(apart), axis=1, keepdims=True) * RANGE).astype(jnp.int32) + 1
    step = reach.astype(F32) * (1.0 / (RANGE * 32767.0))
    level = jnp.round(apart / step).astype(jnp.int32)
    words = pair(level[:, :half], level[:, half:])
    row = lax.broadcasted_iota(jnp.int32, (vecs, size), 0)
    lane = lax.broadcasted_iota(jnp.int32, (vecs, size), 1)
    header = jnp.where(lane == row, mean, jnp.where(lane == row + vecs, reach, 0))
    out_ref[: vecs // 2] = jnp.concatenate([words[: vecs // 2], words[vecs // 2 :]], axis=1)
    out_ref[vecs // 2 :] = jnp.broadcast_to(jnp.sum(header, axis=0, keepdims=True), (8, size))


def decode(block, half):
    words = block[half : block.shape[0] - 8]
    vecs = 2 * words.shape[0]
    level = jnp.concatenate([jnp.concatenate(unpair(part), axis=1) for part in (words[:, :half], words[:, half:])], axis=0)
    header = block[block.shape[0] - 8 :].astype(F32)[:1, : 2 * vecs]
    row = lax.broadcasted_iota(jnp.int32, (vecs, 2 * vecs), 0)
    lane = lax.broadcasted_iota(jnp.int32, (vecs, 2 * vecs), 1)
    mean = jnp.sum(jnp.where(lane == row, header, 0.0), axis=1, keepdims=True) * (1.0 / FIXED)
    step = jnp.sum(jnp.where(lane == row + vecs, header, 0.0), axis=1, keepdims=True) * (1.0 / (RANGE * 32767.0))
    return level.astype(F32) * step + mean


def split_codes(words):
    code = jnp.concatenate(unpair(words), axis=0)
    high = ((code + 128) >> 8) << 8
    return high.astype(F32).astype(BF16), (code - high).astype(F32).astype(BF16)


def kernel_rows(words, own_high, own_low, own_norms, scale):
    high, low = split_codes(words)
    wide = high.astype(F32) + low.astype(F32)
    norms = scale * jnp.sum(wide * wide, axis=1, keepdims=True)
    dots = matmul(high, own_high, (1, 1)) + (matmul(high, own_low, (1, 1)) + matmul(low, own_high, (1, 1))) + matmul(low, own_low, (1, 1))
    return jnp.exp((2.0 * scale) * dots - (norms + own_norms)).astype(BF16)


def own_side(refs, half, scale):
    parts = [split_codes(ref[:half]) for ref in refs]
    high = jnp.concatenate([part[0] for part in parts], axis=0)
    low = jnp.concatenate([part[1] for part in parts], axis=0)
    wide = high.astype(F32) + low.astype(F32)
    norms = matmul(jnp.ones((8, wide.shape[1]), F32), wide * wide, (1, 1), HIGHEST)[:1]
    return high, low, scale * norms


def side_kernel(half, scale, own_ref, outer_ref, high_ref, low_ref, norms_ref):
    high_ref[...], low_ref[...], norms_ref[...] = own_side((own_ref, outer_ref), half, scale)


def build_kernel(half, scale, *refs):
    side, blocks, (tile_ref, start_ref) = refs[:3], refs[3:-2], refs[-2:]
    for b, block in enumerate(blocks):
        place = pl.ds(b * 2 * half, 2 * half)
        tile_ref[place, :] = kernel_rows(block[:half], *(ref[...] for ref in side), scale)
        start_ref[:, place] = decode(block[...], half)


def first_kernel(count, half, scale, total, *refs):
    side, block, tiles, parts = refs[:3], refs[3], refs[4 : 4 + count], refs[4 + count : -2]
    out_ref, tile_ref = refs[-2:]
    size = 2 * half
    tile_ref[...] = kernel_rows(block[:half], *(ref[...] for ref in side), scale)
    starts = [part[...] for part in parts] + [decode(block[...], half)]
    pieces = [start[:, b : b + size] for start in starts for b in range(0, start.shape[1], size)]
    sums = pieces[0]
    for piece in pieces[1:]:
        sums = sums + piece
    mean = jnp.sum(sums, axis=1, keepdims=True) / total
    images = None
    for start, tile in zip(starts, (*tiles, tile_ref)):
        term = matmul((start - mean).astype(BF16), tile[...], (1, 0))
        images = term if images is None else images + term
    out_ref[...] = images


def inverse_factor(gram):
    n = gram.shape[0]
    row_id = lax.broadcasted_iota(jnp.int32, (n, 2 * n), 0)
    col_id = lax.broadcasted_iota(jnp.int32, (n, 2 * n), 1)
    eye = (row_id[:, :n] == col_id[:, :n]).astype(F32)
    work = jnp.concatenate([gram, eye], axis=1)
    done = []
    for top in range(0, n, 8):
        rows = n - top
        place = lax.broadcasted_iota(jnp.int32, (rows, 2 * n), 0)
        columns = [jnp.broadcast_to(work[:, top + k : top + k + 1], (rows, 2 * n)) for k in range(8)]
        for k in range(0, 8, 2):
            one, two = columns[k], columns[k + 1]
            a, b, d = one[k : k + 1], one[k + 1 : k + 2], two[k + 1 : k + 2]
            inverse = 1.0 / a
            slope = b * inverse
            second = jnp.where(place > k + 1, (two * a - one * b) * (1.0 / (a * d - b * b)), 0.0)
            first = jnp.where(place > k, one, 0.0)

            def eliminate(value):
                upper = value[k : k + 1]
                return value - first * (upper * inverse) - second * (value[k + 1 : k + 2] - slope * upper)

            work = eliminate(work)
            columns = columns[: k + 2] + [eliminate(column) for column in columns[k + 2 :]]
        done.append(work[:8])
        work = work[8:]
    upper = jnp.concatenate(done, axis=0)
    pivots = jnp.sum(jnp.where(row_id == col_id, upper, 0.0), axis=1, keepdims=True)
    return upper[:, n:] * lax.rsqrt(pivots)


def thirds(value):
    high = value.astype(BF16)
    rest = value - high.astype(F32)
    middle = rest.astype(BF16)
    return jnp.concatenate([high, middle, (rest - middle.astype(F32)).astype(BF16)], axis=0)


def gram_of(stack):
    n = stack.shape[0] // 3
    p = matmul(stack, stack, (1, 1))
    middle = p[n : 2 * n, n : 2 * n] + (p[:n, 2 * n :] + p[2 * n :, :n])
    return p[:n, :n] + ((p[:n, n : 2 * n] + p[n : 2 * n, :n]) + middle)


def times(matrix, stack):
    n = matrix.shape[0]
    parts = thirds(matrix)
    p = matmul(jnp.concatenate([parts, parts, parts], axis=1), stack, (1, 0))
    return p[:n] + (p[n : 2 * n] + p[2 * n :])


def partial_kernel(count, *refs):
    shift_ref, images = refs[0], refs[1 : 1 + count]
    stack_ref, gram_ref, sum_ref = refs[-3:]
    value = jnp.concatenate([image[...] for image in images], axis=1) - shift_of(shift_ref)
    stack = thirds(value)
    stack_ref[...] = stack
    gram_ref[...] = gram_of(stack)
    sum_ref[...] = jnp.broadcast_to(jnp.sum(value, axis=1, keepdims=True), sum_ref.shape)


def shift_of(ref):
    return jnp.sum(ref[...], axis=1, keepdims=True) * (1.0 / ref.shape[1])


def second_kernel(parts, pieces, total, *refs):
    shift_ref, images = refs[0], refs[1:3]
    stacks, grams, sums = (refs[3 + i * parts : 3 + (i + 1) * parts] for i in range(3))
    tiles = refs[3 + 3 * parts : -3]
    own_ref, other_ref, share_ref = refs[-3:]
    size = own_ref.shape[1]
    value = jnp.concatenate([image[...] for image in images], axis=1) - shift_of(shift_ref)
    stack = thirds(value)
    gram = gram_of(stack)
    far = jnp.sum(value, axis=1, keepdims=True)
    for part, sum_part in zip(grams, sums):
        gram, far = gram + part[...], far + sum_part[:, :1]
    far = far * (1.0 / total)
    n = gram.shape[0]
    eye = lax.broadcasted_iota(jnp.int32, (n, n), 0) == lax.broadcasted_iota(jnp.int32, (n, n), 1)
    row = jnp.sum(jnp.where(eye, far, 0.0), axis=0, keepdims=True)
    gram = gram - (total * far) * row
    solve = math.sqrt(total) * inverse_factor(gram)
    level = jnp.sum(solve * row, axis=1, keepdims=True)
    whole = jnp.concatenate([*(part[...] for part in stacks), stack], axis=1)
    vectors = (times(solve, whole) - level).astype(BF16)
    vectors = jnp.concatenate([vectors[:, p * size : (p + 1) * size] for p in pieces], axis=1)
    result, begin = None, 0
    for tile in tiles:
        end = begin + tile.shape[0]
        term = matmul(vectors[:, begin:end], tile[...], (1, 0))
        result, begin = term if result is None else result + term, end
    own_ref[...] = result[:, :size]
    other_ref[...] = result[:, size:]
    local_mean = jnp.sum(result, axis=1, keepdims=True) / (2 * size)
    gram = gram_of(thirds(result - local_mean))
    h = n // 2
    across = jnp.sum(jnp.where(eye, local_mean, 0.0), axis=0, keepdims=True)
    share_ref[:h] = jnp.concatenate([gram[:h], gram[h:, h:], local_mean[:h], local_mean[h:], jnp.zeros((h, h - 2), F32)], axis=1)
    share_ref[h:] = jnp.broadcast_to(jnp.concatenate([across, across[:, h:], jnp.zeros((1, h), F32)], axis=1), (8, 4 * h))


def merge(a, b, each):
    h = a.shape[0] - 8
    apart = a - b
    lane = lax.broadcasted_iota(jnp.int32, (h, 4 * h), 1)
    down = jnp.where(lane < 2 * h, apart[:h, 3 * h : 3 * h + 1], apart[:h, 3 * h + 1 : 3 * h + 2])
    both = a + b
    top = jnp.where(lane < 3 * h, both[:h] + (0.5 * each) * (down * apart[h : h + 1]), 0.5 * both[:h])
    return jnp.concatenate([top, 0.5 * both[h:]], axis=0)


def merge_kernel(each, a_ref, b_ref, out_ref):
    out_ref[...] = merge(a_ref[...], b_ref[...], each)


def column_kernel(each, outer_ref, share_ref, near_ref, far_ref, across_ref, out_ref):
    outer = outer_ref[0] == 1
    first = jnp.where(outer, near_ref[...], share_ref[...])
    out_ref[...] = merge(first, jnp.where(outer, far_ref[...], across_ref[...]), each)


def last_kernel(total, outer_ref, share_ref, beside_ref, own_ref, given_ref, out_ref):
    images = jnp.where(outer_ref[0] == 1, given_ref[...], own_ref[...])
    share = merge(share_ref[...], beside_ref[...], 0.5 * total)
    h = share.shape[0] - 8
    mean = jnp.concatenate([share[:h, 3 * h : 3 * h + 1], share[:h, 3 * h + 1 : 3 * h + 2]], axis=0)
    top = share[:h, : 2 * h]
    bottom = jnp.concatenate([top[:, h:].T, share[:h, 2 * h : 3 * h]], axis=1)
    solve = math.sqrt(total) * inverse_factor(jnp.concatenate([top, bottom], axis=0))
    out_ref[...] = times(solve, thirds(images - mean))


def call(kernel, args, out_shape, in_specs=None):
    return pl.pallas_call(
        kernel,
        out_shape=out_shape,
        in_specs=in_specs or [VMEM] * len(args),
        out_specs=jax.tree.map(lambda _: VMEM, out_shape),
        compiler_params=pltpu.CompilerParams(vmem_limit_bytes=24 * 2**20),
    )(*args)


def after(value, *others):
    return lax.optimization_barrier((value, *others))[0]


def exchange(axis, offset, size=4):
    return lambda value: lax.ppermute(value, axis, [(i, i ^ offset) for i in range(size)])


CORE, CHIP = exchange("row", 1), exchange("row", 2)
NEAR, FAR, OPPOSITE = exchange("col", 1), exchange("col", 2), exchange("col", 3)


def middle(value):
    return lax.ppermute(value, ("row", "col"), [(4 * r + c, 4 * (r ^ 0) + 3 - c) if c in (1, 2) else (4 * r + c, 4 * (r ^ 1) + c) for r in range(4) for c in range(4)])


def diagonal(value):
    return lax.ppermute(value, ("row", "col"), [(4 * r + c, 4 * (r ^ 2) + 3 - c) if c in (1, 2) else (4 * r + c, 4 * (r ^ 1) + c) for r in range(4) for c in range(4)])


MIDDLE = [(1, 2), (2, 1)]


def local(corpus, sample_rows, initial):
    vecs, size = initial.shape
    half = size // 2
    count = 16
    total = float(size * count)
    scale = UNIT * UNIT / (2.0 * corpus.shape[1])
    levels = call(encode, [initial], jax.ShapeDtypeStruct((vecs // 2 + 8, size), jnp.int32))
    landmarks = lax.gather(
        corpus,
        sample_rows[:, None],
        lax.GatherDimensionNumbers(offset_dims=(1,), collapsed_slice_dims=(0,), start_index_map=(0,)),
        (1, corpus.shape[1]),
        mode="promise_in_bounds",
    )
    code = jnp.round(landmarks * (1.0 / UNIT)).astype(jnp.int32)
    own = jnp.concatenate([pair(code[:half], code[half:]), levels], axis=0)

    def build(*blocks):
        shapes = jax.ShapeDtypeStruct((len(blocks) * size, 2 * size), BF16), jax.ShapeDtypeStruct((vecs, len(blocks) * size), F32)
        tile, start = call(functools.partial(build_kernel, half, scale), [*side, *blocks], shapes)
        tiles.append(tile)
        starts.append(start)

    outer, partner, chip = NEAR(own), middle(own), CHIP(own)
    tiles, starts = [], []
    groups = [[own, outer, CORE(own), CORE(outer)]]
    codes = jax.ShapeDtypeStruct((2 * size, corpus.shape[1]), BF16)
    side = call(functools.partial(side_kernel, half, scale), [own, outer], (codes, codes, jax.ShapeDtypeStruct((1, 2 * size), F32)))
    build(*groups[0])
    partner_outer, chip_outer, chip_partner = middle(outer), NEAR(chip), CHIP(partner)
    groups.append([partner, CORE(partner), chip, CORE(chip)])
    build(*groups[1])
    chip_partner_outer = CHIP(after(partner_outer, tiles[0]))
    build(partner_outer, CORE(partner_outer))
    build(chip_partner, CORE(chip_partner))
    final = CORE(after(chip_partner_outer, *tiles[1:5]))
    build(chip_outer, CORE(chip_outer))
    build(chip_partner_outer)
    images, tile = call(
        functools.partial(first_kernel, len(tiles), half, scale, total),
        [*side, final, *tiles, *starts],
        (jax.ShapeDtypeStruct((vecs, 2 * size), F32), jax.ShapeDtypeStruct((size, 2 * size), BF16)),
    )
    tiles.append(tile)
    places = [images, middle(images), CHIP(images), diagonal(images)]
    pairs = [[value, CORE(value)] for value in places]
    block = jax.ShapeDtypeStruct((vecs, size), F32)
    parts = []
    for group in ([0, 1, 2],):
        values = [value for p in group for value in pairs[p]]
        shapes = jax.ShapeDtypeStruct((3 * vecs, len(values) * 2 * size), BF16), jax.ShapeDtypeStruct((vecs, vecs), F32)
        parts.append(call(functools.partial(partial_kernel, len(values)), [images, *values], (*shapes, jax.ShapeDtypeStruct((vecs, 128), F32))))
    here, part, chip, far = (4 * p for p in range(4))
    pieces = [here, here + 1, here + 2, here + 3, part, part + 2, chip, chip + 2]
    pieces += [part + 1, part + 3, far, far + 2, chip + 1, chip + 3, far + 1, far + 3]
    packed = jax.ShapeDtypeStruct((vecs // 2 + 8, 2 * vecs), F32)
    known = [part[i] for i in range(3) for part in parts]
    images, other, share = call(
        functools.partial(second_kernel, len(parts), pieces, total), [images, *pairs[3], *known, *tiles], (block, block, packed)
    )
    given = NEAR(other)
    place = lax.axis_index("col")
    flag = ((place == 0) | (place == 3)).astype(jnp.int32).reshape(1)
    share = call(functools.partial(merge_kernel, 2.0 * size), [share, CORE(share)], packed)
    smem = pl.BlockSpec(memory_space=pltpu.SMEM)
    share = call(
        functools.partial(column_kernel, 4.0 * size),
        [flag, share, NEAR(share), lax.ppermute(share, "col", [(0, 1), (1, 3), (2, 0), (3, 2)]), middle(share)],
        packed,
        [smem] + [VMEM] * 4,
    )
    return call(functools.partial(last_kernel, total), [flag, share, CHIP(share), images, given], block, [smem] + [VMEM] * 4)


def local_large(corpus, sample_rows, initial):
    both = ("row", "col")
    landmarks = corpus[sample_rows]
    everyone = lax.all_gather(landmarks, both, axis=0, tiled=True)
    total = float(everyone.shape[0])
    norms = jnp.sum(everyone * everyone, axis=1)
    own_norms = jnp.sum(landmarks * landmarks, axis=1)
    products = jnp.dot(everyone, landmarks.T, precision=HIGHEST, preferred_element_type=F32)
    tile = jnp.exp(-(norms[:, None] + own_norms[None, :] - 2.0 * products) / (2.0 * corpus.shape[1])).astype(BF16)
    starts = lax.all_gather(initial, both, axis=1, tiled=True)
    rounded = (starts - jnp.mean(starts, axis=1, keepdims=True)).astype(BF16)
    vectors = None
    for _ in range(ITERS):
        images = jnp.dot(rounded, tile, preferred_element_type=F32)
        gathered = lax.all_gather(images, both, axis=1, tiled=True)
        mean = jnp.mean(gathered, axis=1, keepdims=True)
        centered = gathered - mean
        factor = jnp.linalg.cholesky(jnp.dot(centered, centered.T, precision=HIGHEST))
        rounded = (math.sqrt(total) * jax.scipy.linalg.solve_triangular(factor, centered, lower=True)).astype(BF16)
        vectors = math.sqrt(total) * jax.scipy.linalg.solve_triangular(factor, images - mean, lower=True)
    return vectors


def solution(mesh):
    shape = mesh.shape
    whole = P(("groups", "row", "col"))
    return jax.shard_map(
        local if (shape["row"], shape["col"]) == (4, 4) else local_large,
        mesh=mesh,
        in_specs=(P(("groups", "row", "col"), None), whole, P(None, ("groups", "row", "col"))),
        out_specs=P(None, ("groups", "row", "col")),
        check_vma=False,
    )
```

```python
import functools
import math

import jax
import jax.numpy as jnp
from jax import lax
from jax.experimental import pallas as pl
from jax.experimental.pallas import tpu as pltpu
from jax.sharding import PartitionSpec as P

ITERS = 2
REACH = 20.0
UNIT = REACH / 32767.0
FIXED, RANGE = 2.0**28, 2.0**26
HIGHEST = lax.Precision.HIGHEST
BF16, F32 = jnp.bfloat16, jnp.float32
VMEM = pl.BlockSpec(memory_space=pltpu.VMEM)


def matmul(a, b, contract, precision=None):
    return lax.dot_general(a, b, ((contract[:1], contract[1:]), ((), ())), precision=precision, preferred_element_type=F32)


def pair(high, low):
    return (high << 16) | (low & 0xFFFF)


def unpair(words):
    return words >> 16, (words << 16) >> 16


def encode(initial_ref, out_ref):
    initial = initial_ref[...]
    vecs, size = initial.shape
    half = size // 2
    mean = jnp.round(jnp.sum(initial, axis=1, keepdims=True) * (FIXED / size)).astype(jnp.int32)
    apart = initial - mean.astype(F32) * (1.0 / FIXED)
    reach = jnp.ceil(jnp.max(jnp.abs(apart), axis=1, keepdims=True) * RANGE).astype(jnp.int32) + 1
    step = reach.astype(F32) * (1.0 / (RANGE * 32767.0))
    level = jnp.round(apart / step).astype(jnp.int32)
    words = pair(level[:, :half], level[:, half:])
    row = lax.broadcasted_iota(jnp.int32, (vecs, size), 0)
    lane = lax.broadcasted_iota(jnp.int32, (vecs, size), 1)
    header = jnp.where(lane == row, mean, jnp.where(lane == row + vecs, reach, 0))
    out_ref[: vecs // 2] = jnp.concatenate([words[: vecs // 2], words[vecs // 2 :]], axis=1)
    out_ref[vecs // 2 :] = jnp.broadcast_to(jnp.sum(header, axis=0, keepdims=True), (8, size))


def decode(block, half):
    words = block[half : block.shape[0] - 8]
    vecs = 2 * words.shape[0]
    level = jnp.concatenate([jnp.concatenate(unpair(part), axis=1) for part in (words[:, :half], words[:, half:])], axis=0)
    header = block[block.shape[0] - 8 :].astype(F32)[:1, : 2 * vecs]
    row = lax.broadcasted_iota(jnp.int32, (vecs, 2 * vecs), 0)
    lane = lax.broadcasted_iota(jnp.int32, (vecs, 2 * vecs), 1)
    mean = jnp.sum(jnp.where(lane == row, header, 0.0), axis=1, keepdims=True) * (1.0 / FIXED)
    step = jnp.sum(jnp.where(lane == row + vecs, header, 0.0), axis=1, keepdims=True) * (1.0 / (RANGE * 32767.0))
    return level.astype(F32) * step + mean


def split_codes(words):
    code = jnp.concatenate(unpair(words), axis=0)
    high = ((code + 128) >> 8) << 8
    return high.astype(F32).astype(BF16), (code - high).astype(F32).astype(BF16)


def kernel_rows(words, own_high, own_low, own_norms, scale):
    high, low = split_codes(words)
    wide = high.astype(F32) + low.astype(F32)
    norms = scale * jnp.sum(wide * wide, axis=1, keepdims=True)
    dots = matmul(high, own_high, (1, 1)) + (matmul(high, own_low, (1, 1)) + matmul(low, own_high, (1, 1))) + matmul(low, own_low, (1, 1))
    return jnp.exp((2.0 * scale) * dots - (norms + own_norms)).astype(BF16)


def own_side(refs, half, scale):
    parts = [split_codes(ref[:half]) for ref in refs]
    high = jnp.concatenate([part[0] for part in parts], axis=0)
    low = jnp.concatenate([part[1] for part in parts], axis=0)
    wide = high.astype(F32) + low.astype(F32)
    norms = matmul(jnp.ones((8, wide.shape[1]), F32), wide * wide, (1, 1), HIGHEST)[:1]
    return high, low, scale * norms


def side_kernel(half, scale, own_ref, outer_ref, high_ref, low_ref, norms_ref):
    high_ref[...], low_ref[...], norms_ref[...] = own_side((own_ref, outer_ref), half, scale)


def build_kernel(half, scale, *refs):
    side, blocks, (tile_ref, start_ref) = refs[:3], refs[3:-2], refs[-2:]
    for b, block in enumerate(blocks):
        place = pl.ds(b * 2 * half, 2 * half)
        tile_ref[place, :] = kernel_rows(block[:half], *(ref[...] for ref in side), scale)
        start_ref[:, place] = decode(block[...], half)


def first_kernel(count, half, scale, total, *refs):
    side, block, tiles, parts = refs[:3], refs[3], refs[4 : 4 + count], refs[4 + count : -2]
    out_ref, tile_ref = refs[-2:]
    size = 2 * half
    tile_ref[...] = kernel_rows(block[:half], *(ref[...] for ref in side), scale)
    starts = [part[...] for part in parts] + [decode(block[...], half)]
    pieces = [start[:, b : b + size] for start in starts for b in range(0, start.shape[1], size)]
    sums = pieces[0]
    for piece in pieces[1:]:
        sums = sums + piece
    mean = jnp.sum(sums, axis=1, keepdims=True) / total
    images = None
    for start, tile in zip(starts, (*tiles, tile_ref)):
        term = matmul((start - mean).astype(BF16), tile[...], (1, 0))
        images = term if images is None else images + term
    out_ref[...] = images


def inverse_factor(gram):
    n = gram.shape[0]
    row_id = lax.broadcasted_iota(jnp.int32, (n, 2 * n), 0)
    col_id = lax.broadcasted_iota(jnp.int32, (n, 2 * n), 1)
    eye = (row_id[:, :n] == col_id[:, :n]).astype(F32)
    work = jnp.concatenate([gram, eye], axis=1)
    done = []
    for top in range(0, n, 8):
        rows = n - top
        place = lax.broadcasted_iota(jnp.int32, (rows, 2 * n), 0)
        columns = [jnp.broadcast_to(work[:, top + k : top + k + 1], (rows, 2 * n)) for k in range(8)]
        for k in range(0, 8, 2):
            one, two = columns[k], columns[k + 1]
            a, b, d = one[k : k + 1], one[k + 1 : k + 2], two[k + 1 : k + 2]
            inverse = 1.0 / a
            slope = b * inverse
            second = jnp.where(place > k + 1, (two * a - one * b) * (1.0 / (a * d - b * b)), 0.0)
            first = jnp.where(place > k, one, 0.0)

            def eliminate(value):
                upper = value[k : k + 1]
                return value - first * (upper * inverse) - second * (value[k + 1 : k + 2] - slope * upper)

            work = eliminate(work)
            columns = columns[: k + 2] + [eliminate(column) for column in columns[k + 2 :]]
        done.append(work[:8])
        work = work[8:]
    upper = jnp.concatenate(done, axis=0)
    pivots = jnp.sum(jnp.where(row_id == col_id, upper, 0.0), axis=1, keepdims=True)
    return upper[:, n:] * lax.rsqrt(pivots)


def thirds(value):
    high = value.astype(BF16)
    rest = value - high.astype(F32)
    middle = rest.astype(BF16)
    return jnp.concatenate([high, middle, (rest - middle.astype(F32)).astype(BF16)], axis=0)


def gram_of(stack):
    n = stack.shape[0] // 3
    p = matmul(stack, stack, (1, 1))
    middle = p[n : 2 * n, n : 2 * n] + (p[:n, 2 * n :] + p[2 * n :, :n])
    return p[:n, :n] + ((p[:n, n : 2 * n] + p[n : 2 * n, :n]) + middle)


def times(matrix, stack):
    n = matrix.shape[0]
    parts = thirds(matrix)
    p = matmul(jnp.concatenate([parts, parts, parts], axis=1), stack, (1, 0))
    return p[:n] + (p[n : 2 * n] + p[2 * n :])


def partial_kernel(count, *refs):
    shift_ref, images = refs[0], refs[1 : 1 + count]
    stack_ref, gram_ref, sum_ref = refs[-3:]
    value = jnp.concatenate([image[...] for image in images], axis=1) - shift_of(shift_ref)
    stack = thirds(value)
    stack_ref[...] = stack
    gram_ref[...] = gram_of(stack)
    sum_ref[...] = jnp.broadcast_to(jnp.sum(value, axis=1, keepdims=True), sum_ref.shape)


def shift_of(ref):
    return jnp.sum(ref[...], axis=1, keepdims=True) * (1.0 / ref.shape[1])


def second_kernel(parts, pieces, total, *refs):
    shift_ref, images = refs[0], refs[1:3]
    stacks, grams, sums = (refs[3 + i * parts : 3 + (i + 1) * parts] for i in range(3))
    tiles = refs[3 + 3 * parts : -3]
    own_ref, other_ref, share_ref = refs[-3:]
    size = own_ref.shape[1]
    value = jnp.concatenate([image[...] for image in images], axis=1) - shift_of(shift_ref)
    stack = thirds(value)
    gram = gram_of(stack)
    far = jnp.sum(value, axis=1, keepdims=True)
    for part, sum_part in zip(grams, sums):
        gram, far = gram + part[...], far + sum_part[:, :1]
    far = far * (1.0 / total)
    n = gram.shape[0]
    eye = lax.broadcasted_iota(jnp.int32, (n, n), 0) == lax.broadcasted_iota(jnp.int32, (n, n), 1)
    row = jnp.sum(jnp.where(eye, far, 0.0), axis=0, keepdims=True)
    gram = gram - (total * far) * row
    solve = math.sqrt(total) * inverse_factor(gram)
    level = jnp.sum(solve * row, axis=1, keepdims=True)
    whole = jnp.concatenate([*(part[...] for part in stacks), stack], axis=1)
    vectors = (times(solve, whole) - level).astype(BF16)
    vectors = jnp.concatenate([vectors[:, p * size : (p + 1) * size] for p in pieces], axis=1)
    result, begin = None, 0
    for tile in tiles:
        end = begin + tile.shape[0]
        term = matmul(vectors[:, begin:end], tile[...], (1, 0))
        result, begin = term if result is None else result + term, end
    own_ref[...] = result[:, :size]
    other_ref[...] = result[:, size:]
    local_mean = jnp.sum(result, axis=1, keepdims=True) / (2 * size)
    gram = gram_of(thirds(result - local_mean))
    h = n // 2
    across = jnp.sum(jnp.where(eye, local_mean, 0.0), axis=0, keepdims=True)
    share_ref[:h] = jnp.concatenate([gram[:h], gram[h:, h:], local_mean[:h], local_mean[h:], jnp.zeros((h, h - 2), F32)], axis=1)
    share_ref[h:] = jnp.broadcast_to(jnp.concatenate([across, across[:, h:], jnp.zeros((1, h), F32)], axis=1), (8, 4 * h))


def merge(a, b, each):
    h = a.shape[0] - 8
    apart = a - b
    lane = lax.broadcasted_iota(jnp.int32, (h, 4 * h), 1)
    down = jnp.where(lane < 2 * h, apart[:h, 3 * h : 3 * h + 1], apart[:h, 3 * h + 1 : 3 * h + 2])
    both = a + b
    top = jnp.where(lane < 3 * h, both[:h] + (0.5 * each) * (down * apart[h : h + 1]), 0.5 * both[:h])
    return jnp.concatenate([top, 0.5 * both[h:]], axis=0)


def merge_kernel(each, a_ref, b_ref, out_ref):
    out_ref[...] = merge(a_ref[...], b_ref[...], each)


def column_kernel(each, outer_ref, share_ref, near_ref, far_ref, across_ref, out_ref):
    outer = outer_ref[0] == 1
    first = jnp.where(outer, near_ref[...], share_ref[...])
    out_ref[...] = merge(first, jnp.where(outer, far_ref[...], across_ref[...]), each)


def last_kernel(total, outer_ref, share_ref, beside_ref, own_ref, given_ref, out_ref):
    images = jnp.where(outer_ref[0] == 1, given_ref[...], own_ref[...])
    share = merge(share_ref[...], beside_ref[...], 0.5 * total)
    h = share.shape[0] - 8
    mean = jnp.concatenate([share[:h, 3 * h : 3 * h + 1], share[:h, 3 * h + 1 : 3 * h + 2]], axis=0)
    top = share[:h, : 2 * h]
    bottom = jnp.concatenate([top[:, h:].T, share[:h, 2 * h : 3 * h]], axis=1)
    solve = math.sqrt(total) * inverse_factor(jnp.concatenate([top, bottom], axis=0))
    out_ref[...] = times(solve, thirds(images - mean))


def call(kernel, args, out_shape, in_specs=None):
    return pl.pallas_call(
        kernel,
        out_shape=out_shape,
        in_specs=in_specs or [VMEM] * len(args),
        out_specs=jax.tree.map(lambda _: VMEM, out_shape),
        compiler_params=pltpu.CompilerParams(vmem_limit_bytes=24 * 2**20),
    )(*args)


def after(value, *others):
    return lax.optimization_barrier((value, *others))[0]


def exchange(axis, offset, size=4):
    return lambda value: lax.ppermute(value, axis, [(i, i ^ offset) for i in range(size)])


CORE, CHIP = exchange("row", 1), exchange("row", 2)
NEAR, FAR, OPPOSITE = exchange("col", 1), exchange("col", 2), exchange("col", 3)


def middle(value):
    return lax.ppermute(value, ("row", "col"), [(4 * r + c, 4 * (r ^ 0) + 3 - c) if c in (1, 2) else (4 * r + c, 4 * (r ^ 1) + c) for r in range(4) for c in range(4)])


def diagonal(value):
    return lax.ppermute(value, ("row", "col"), [(4 * r + c, 4 * (r ^ 2) + 3 - c) if c in (1, 2) else (4 * r + c, 4 * (r ^ 1) + c) for r in range(4) for c in range(4)])


MIDDLE = [(1, 2), (2, 1)]


def local(corpus, sample_rows, initial):
    vecs, size = initial.shape
    half = size // 2
    count = 16
    total = float(size * count)
    scale = UNIT * UNIT / (2.0 * corpus.shape[1])
    levels = call(encode, [initial], jax.ShapeDtypeStruct((vecs // 2 + 8, size), jnp.int32))
    landmarks = lax.gather(
        corpus,
        sample_rows[:, None],
        lax.GatherDimensionNumbers(offset_dims=(1,), collapsed_slice_dims=(0,), start_index_map=(0,)),
        (1, corpus.shape[1]),
        mode="promise_in_bounds",
    )
    code = jnp.round(landmarks * (1.0 / UNIT)).astype(jnp.int32)
    own = jnp.concatenate([pair(code[:half], code[half:]), levels], axis=0)

    def build(*blocks):
        shapes = jax.ShapeDtypeStruct((len(blocks) * size, 2 * size), BF16), jax.ShapeDtypeStruct((vecs, len(blocks) * size), F32)
        tile, start = call(functools.partial(build_kernel, half, scale), [*side, *blocks], shapes)
        tiles.append(tile)
        starts.append(start)

    outer, partner, chip = NEAR(own), middle(own), CHIP(own)
    tiles, starts = [], []
    groups = [[own, outer, CORE(own), CORE(outer)]]
    codes = jax.ShapeDtypeStruct((2 * size, corpus.shape[1]), BF16)
    side = call(functools.partial(side_kernel, half, scale), [own, outer], (codes, codes, jax.ShapeDtypeStruct((1, 2 * size), F32)))
    build(*groups[0])
    partner_outer, chip_outer, chip_partner = middle(outer), NEAR(chip), CHIP(partner)
    groups.append([partner, CORE(partner), chip, CORE(chip)])
    build(*groups[1])
    chip_partner_outer = CHIP(after(partner_outer, tiles[0]))
    build(partner_outer, CORE(partner_outer))
    build(chip_partner)
    build(CORE(chip_partner))
    final = CORE(after(chip_partner_outer, *tiles[1:6]))
    build(chip_outer, CORE(chip_outer))
    build(chip_partner_outer)
    images, tile = call(
        functools.partial(first_kernel, len(tiles), half, scale, total),
        [*side, final, *tiles, *starts],
        (jax.ShapeDtypeStruct((vecs, 2 * size), F32), jax.ShapeDtypeStruct((size, 2 * size), BF16)),
    )
    tiles.append(tile)
    places = [images, middle(images), CHIP(images), diagonal(images)]
    pairs = [[value, CORE(value)] for value in places]
    block = jax.ShapeDtypeStruct((vecs, size), F32)
    parts = []
    for group in ([0, 1, 2],):
        values = [value for p in group for value in pairs[p]]
        shapes = jax.ShapeDtypeStruct((3 * vecs, len(values) * 2 * size), BF16), jax.ShapeDtypeStruct((vecs, vecs), F32)
        parts.append(call(functools.partial(partial_kernel, len(values)), [images, *values], (*shapes, jax.ShapeDtypeStruct((vecs, 128), F32))))
    here, part, chip, far = (4 * p for p in range(4))
    pieces = [here, here + 1, here + 2, here + 3, part, part + 2, chip, chip + 2]
    pieces += [part + 1, part + 3, far, far + 2, chip + 1, chip + 3, far + 1, far + 3]
    packed = jax.ShapeDtypeStruct((vecs // 2 + 8, 2 * vecs), F32)
    known = [part[i] for i in range(3) for part in parts]
    images, other, share = call(
        functools.partial(second_kernel, len(parts), pieces, total), [images, *pairs[3], *known, *tiles], (block, block, packed)
    )
    given = NEAR(other)
    place = lax.axis_index("col")
    flag = ((place == 0) | (place == 3)).astype(jnp.int32).reshape(1)
    share = call(functools.partial(merge_kernel, 2.0 * size), [share, CORE(share)], packed)
    smem = pl.BlockSpec(memory_space=pltpu.SMEM)
    share = call(
        functools.partial(column_kernel, 4.0 * size),
        [flag, share, NEAR(share), lax.ppermute(share, "col", [(0, 1), (1, 3), (2, 0), (3, 2)]), middle(share)],
        packed,
        [smem] + [VMEM] * 4,
    )
    return call(functools.partial(last_kernel, total), [flag, share, CHIP(share), images, given], block, [smem] + [VMEM] * 4)


def local_large(corpus, sample_rows, initial):
    both = ("row", "col")
    landmarks = corpus[sample_rows]
    everyone = lax.all_gather(landmarks, both, axis=0, tiled=True)
    total = float(everyone.shape[0])
    norms = jnp.sum(everyone * everyone, axis=1)
    own_norms = jnp.sum(landmarks * landmarks, axis=1)
    products = jnp.dot(everyone, landmarks.T, precision=HIGHEST, preferred_element_type=F32)
    tile = jnp.exp(-(norms[:, None] + own_norms[None, :] - 2.0 * products) / (2.0 * corpus.shape[1])).astype(BF16)
    starts = lax.all_gather(initial, both, axis=1, tiled=True)
    rounded = (starts - jnp.mean(starts, axis=1, keepdims=True)).astype(BF16)
    vectors = None
    for _ in range(ITERS):
        images = jnp.dot(rounded, tile, preferred_element_type=F32)
        gathered = lax.all_gather(images, both, axis=1, tiled=True)
        mean = jnp.mean(gathered, axis=1, keepdims=True)
        centered = gathered - mean
        factor = jnp.linalg.cholesky(jnp.dot(centered, centered.T, precision=HIGHEST))
        rounded = (math.sqrt(total) * jax.scipy.linalg.solve_triangular(factor, centered, lower=True)).astype(BF16)
        vectors = math.sqrt(total) * jax.scipy.linalg.solve_triangular(factor, images - mean, lower=True)
    return vectors


def solution(mesh):
    shape = mesh.shape
    whole = P(("groups", "row", "col"))
    return jax.shard_map(
        local if (shape["row"], shape["col"]) == (4, 4) else local_large,
        mesh=mesh,
        in_specs=(P(("groups", "row", "col"), None), whole, P(None, ("groups", "row", "col"))),
        out_specs=P(None, ("groups", "row", "col")),
        check_vma=False,
    )
```
